32 devices in a mesh: section: 2 (over core), fsdp: 16 (over z, y, x).
Axes of the slice: x: 2, y: 2, z: 4, core: 2. Of those that a mesh axis runs over, the one named last changes fastest.
Arguments:
- token_ids: int32 [2, 16, 128], P('section', 'fsdp'), may hold values from 0 to 50303
- target_ids: int32 [2, 16, 128], P('section', 'fsdp'), may hold values from 0 to 50303
- true_counts: int32 [2, 16], replicated, may hold values from 32 to 128, as said below
- embed_table: float32 [50304, 768], P('fsdp')
- embed_m: float32 [50304, 768], P('fsdp'), may hold values from -1.9073486e-06 to 1.9073486e-06
- embed_v: float32 [50304, 768], P('fsdp'), may hold values from 6.3649325e-12 to 2.5535503e-11
- pos_table: float32 [128, 768], P(None, 'fsdp'), may hold values from -1.75 to 1.75
- pos_m: float32 [128, 768], P(None, 'fsdp'), may hold values from -1.9073486e-06 to 1.9073486e-06
- pos_v: float32 [128, 768], P(None, 'fsdp'), may hold values from 3.98566e-13 to 1.594264e-12
- w_qkv: float32 [2, 768, 2304], P('section', None, 'fsdp'), may hold values from -0.21875 to 0.21875
- w_proj: float32 [2, 768, 768], P('section', None, 'fsdp'), may hold values from -0.4375 to 0.4375
- w_fc: float32 [2, 768, 3072], P('section', None, 'fsdp'), may hold values from -0.21875 to 0.21875
- w_down: float32 [2, 768, 3072], P('section', None, 'fsdp'), may hold values from -0.109375 to 0.109375
- mom_qkv: float32 [2, 768, 2304], P('section', None, 'fsdp'), may hold values from -1.5258789e-05 to 1.5258789e-05
- mom_proj: float32 [2, 768, 768], P('section', None, 'fsdp'), may hold values from -1.5258789e-05 to 1.5258789e-05
- mom_fc: float32 [2, 768, 3072], P('section', None, 'fsdp'), may hold values from -1.5258789e-05 to 1.5258789e-05
- mom_down: float32 [2, 768, 3072], P('section', None, 'fsdp'), may hold values from -1.5258789e-05 to 1.5258789e-05
- layer_vecs: float32 [2, 12, 768], P('section', None, 'fsdp')
- vecs_m: float32 [2, 12, 768], P('section', None, 'fsdp'), may hold values from -9.536743e-06 to 9.536743e-06
- vecs_v: float32 [2, 12, 768], P('section', None, 'fsdp'), may hold values from 9.96415e-12 to 3.98566e-11
- final_norm: float32 [2, 768], P(None, 'fsdp')
- norm_m: float32 [2, 768], P(None, 'fsdp'), may hold values from -9.536743e-06 to 9.536743e-06
- norm_v: float32 [2, 768], P(None, 'fsdp'), may hold values from 9.96415e-12 to 3.98566e-11
Outputs:
- loss_sum: float32 [], replicated
- clip_norm: float32 [], replicated
- embed_new: float32 [50304, 768], P('fsdp')
- embed_low: bfloat16 [50304, 768], P('fsdp')
- embed_m_new: float32 [50304, 768], P('fsdp')
- embed_v_new: float32 [50304, 768], P('fsdp')
- pos_new: float32 [128, 768], P(None, 'fsdp')
- pos_m_new: float32 [128, 768], P(None, 'fsdp')
- pos_v_new: float32 [128, 768], P(None, 'fsdp')
- qkv_new: float32 [2, 768, 2304], P('section', None, 'fsdp')
- qkv_low: bfloat16 [2, 768, 2304], P('section', None, 'fsdp')
- qkv_mom: float32 [2, 768, 2304], P('section', None, 'fsdp')
- proj_new: float32 [2, 768, 768], P('section', None, 'fsdp')
- proj_low: bfloat16 [2, 768, 768], P('section', None, 'fsdp')
- proj_mom: float32 [2, 768, 768], P('section', None, 'fsdp')
- fc_new: float32 [2, 768, 3072], P('section', None, 'fsdp')
- fc_low: bfloat16 [2, 768, 3072], P('section', None, 'fsdp')
- fc_mom: float32 [2, 768, 3072], P('section', None, 'fsdp')
- down_new: float32 [2, 768, 3072], P('section', None, 'fsdp')
- down_low: bfloat16 [2, 768, 3072], P('section', None, 'fsdp')
- down_mom: float32 [2, 768, 3072], P('section', None, 'fsdp')
- vecs_new: float32 [2, 12, 768], P('section', None, 'fsdp')
- vecs_m_new: float32 [2, 12, 768], P('section', None, 'fsdp')
- vecs_v_new: float32 [2, 12, 768], P('section', None, 'fsdp')
- norm_new: float32 [2, 768], P(None, 'fsdp')
- norm_m_new: float32 [2, 768], P(None, 'fsdp')
- norm_v_new: float32 [2, 768], P(None, 'fsdp')
The draws below stay inside these ranges and needn't reach their ends.
Inputs may be any that keep to these rules, and one draw needn't show every extreme that they name: `true_counts`: leading positions of a sequence that count in the loss; the last sequence of each micro-batch counts all 128.
All inputs are finite; a program needn't handle non-finite values.
Results may differ from the reference program's by a relative error of at most 0.0075.
The reference program's roundings to bfloat16 on the way (of `table`, `normed_a`, `qkv`, `attended` and `hidden`) count: a program that leaves them out, or rounds other values in their place, can miss the bound.
Values may be sent and summed in bfloat16 or wider, within the bound.
No kernel may reach another device: no remote copies, remote signals or barrier semaphores. Data moves between devices by JAX's collectives and lax.ppermute only.
A program may use at most 168 MiB of HBM per device.

```python
import math
import jax
import jax.numpy as jnp
import numpy as np
from jax import lax

D = 768
HD = 64
FF = 3072
VOCAB = 50304
SEQ = 128
STEP = 10
SEQS = 16
MB = 2
LAYERS = 2


def rising_gains(factors, bias_draw, gain_rows, floor_value):
    columns = jnp.arange(D, dtype=jnp.float32) / D
    return jnp.where(gain_rows, (floor_value + columns) * factors, bias_draw)


def draw_true_counts(key, part):
    key = jax.random.fold_in(key, 11)
    columns = jnp.arange(SEQS, dtype=jnp.int32)
    ceiling = SEQ // 3 + (SEQ - SEQ // 3) * columns // max(SEQS - 1, 1)
    cuts = jax.random.randint(key, (MB, SEQS), 0, 1 << 20) % (ceiling // 4 + 1)[None, :]
    counts = ceiling[None, :] - cuts
    counts = counts.at[:, SEQS - 1].set(SEQ)
    counts = counts.at[0, 0].set(SEQ // 3 - SEQ // 3 // 4)
    return counts.astype(jnp.int32)


def draw_embed_table(key, part):
    key = jax.random.fold_in(key, 12)
    rows_at = jnp.arange(VOCAB, dtype=jnp.float32)[:, None] / VOCAB
    base_draw = jnp.clip(jax.random.normal(key, (VOCAB, D), jnp.float32), -5.0, 5.0)
    spread = 1.0 + 2.0 * rows_at
    return base_draw * spread / jnp.sqrt(jnp.float32(D))


def draw_layer_vecs(key, part):
    key = jax.random.fold_in(key, 13)
    first_key, second_key = jax.random.split(key)
    full_shape = (LAYERS, 12, D)
    row_ids = jnp.arange(12)[None, :, None]
    gain_rows = (row_ids == 0) | (row_ids == 5)
    factors = jax.random.uniform(first_key, full_shape, jnp.float32, 0.8, 1.2)
    bias_draw = 0.2 * jax.random.normal(second_key, full_shape, jnp.float32)
    return rising_gains(factors, bias_draw, gain_rows, 0.5)


def draw_final_norm(key, part):
    key = jax.random.fold_in(key, 14)
    first_key, second_key = jax.random.split(key)
    full_shape = (2, D)
    gain_rows = jnp.arange(2)[:, None] == 0
    factors = jax.random.uniform(first_key, full_shape, jnp.float32, 0.8, 1.2)
    bias_draw = 0.2 * jax.random.normal(second_key, full_shape, jnp.float32)
    return rising_gains(factors, bias_draw, gain_rows, 0.5)


def touch_ends(drawn, rng, low, high):
    shape = drawn.shape
    index_at = [jax.random.randint(jax.random.fold_in(rng, axis), (), 0, shape[axis]) for axis in range(len(shape))]
    drawn = drawn.at[tuple(index_at)].set(low)
    longest = shape.index(max(shape))
    index_at[longest] = (index_at[longest] + 1) % shape[longest]
    return drawn.at[tuple(index_at)].set(high)


def steps_of(own_key, dims, shards, smallest, high):
    def one(dim, parts):
        heights = jax.random.uniform(jax.random.fold_in(jax.random.fold_in(own_key, 6), dim), (parts,), jnp.float32, smallest / len(shards), high / len(shards))
        return jnp.repeat(jnp.exp(heights), dims[dim] // parts).reshape((-1,) + (1,) * (len(dims) - dim - 1))

    loudness = one(*shards[0])
    for cut in shards[1:]:
        loudness = loudness * one(*cut)
    return loudness


def rank_bounds(number_of, skew):
    weights = [(1 << 20) // math.isqrt(rank ** skew) + 1 for rank in range(1, number_of + 1)]
    width = 1 + sum(weights) // (1 << 30)
    return np.cumsum(np.array([max(1, weight // width) for weight in weights]))


def skewed_ids(own_key, dims, count, lean):
    table = rank_bounds(count, lean)
    pick = jax.random.randint(jax.random.fold_in(own_key, 1), dims, 0, int(table[count - 1]))
    standing = jnp.searchsorted(jnp.asarray(table, jnp.int32), pick, side="right")
    return jax.random.permutation(jax.random.fold_in(own_key, 2), count)[standing].astype(jnp.int32)


def gaussian(own_key, dims, width, most, cuts=(), kind=jnp.bfloat16):
    level = steps_of(own_key, dims, cuts, -0.22, 0.18) if cuts else 1.0
    array = jax.random.normal(own_key, dims, jnp.float32) * width * level
    return jnp.minimum(jnp.maximum(array, -most), most).astype(kind)


def setup_inputs(seed: int = 0) -> dict:
    seeds = jax.random.split(jax.random.key(seed), 24)
    return {
        "token_ids": touch_ends(skewed_ids(seeds[0], (MB, SEQS, SEQ), VOCAB, 2), jax.random.fold_in(seeds[0], 3), 0, VOCAB - 1).astype(jnp.int32),
        "target_ids": touch_ends(skewed_ids(seeds[1], (MB, SEQS, SEQ), VOCAB, 2), jax.random.fold_in(seeds[1], 3), 0, VOCAB - 1).astype(jnp.int32),
        "true_counts": draw_true_counts(jax.random.fold_in(seeds[23], 71), 0),
        "embed_table": draw_embed_table(jax.random.fold_in(seeds[23], 71), 0),
        "embed_m": gaussian(seeds[4], (VOCAB, D), (0.111 * 0.02 * (VOCAB * D + 24 * D * D) ** -0.5), 1.9073486328125e-06, ((0, 16),), jnp.float32),
        "embed_v": jnp.clip(jnp.exp(math.log(2.5535502531925935e-11) - 1.3892661 * jax.random.uniform(seeds[5], (VOCAB, D), jnp.float32) ** steps_of(seeds[5], (VOCAB, D), ((0, 16),), -0.2, 0.2)), 6.364932452623817e-12, 2.5535502531925935e-11),
        "pos_table": gaussian(seeds[6], (SEQ, D), 0.3, 1.75, ((1, 16),), jnp.float32),
        "pos_m": gaussian(seeds[7], (SEQ, D), (0.111 * 0.02 * (VOCAB * D + 24 * D * D) ** -0.5), 1.9073486328125e-06, ((1, 16),), jnp.float32),
        "pos_v": jnp.clip(jnp.exp(math.log(1.5942640003291375e-12) - 1.3862944 * jax.random.uniform(seeds[8], (SEQ, D), jnp.float32) ** steps_of(seeds[8], (SEQ, D), ((1, 16),), -0.2, 0.2)), 3.985660000822844e-13, 1.5942640003291375e-12),
        "w_qkv": gaussian(seeds[9], (LAYERS, D, 3 * D), D ** -0.5, 0.21875, ((0, 2), (2, 16)), jnp.float32),
        "w_proj": gaussian(seeds[10], (LAYERS, D, D), (D // 4) ** -0.5, 0.4375, ((0, 2), (2, 16)), jnp.float32),
        "w_fc": gaussian(seeds[11], (LAYERS, D, FF), D ** -0.5, 0.21875, ((0, 2), (2, 16)), jnp.float32),
        "w_down": gaussian(seeds[12], (LAYERS, D, FF), FF ** -0.5, 0.109375, ((0, 2), (2, 16)), jnp.float32),
        "mom_qkv": gaussian(seeds[13], (LAYERS, D, 3 * D), (0.02 * (VOCAB * D + 24 * D * D) ** -0.5), 1.52587890625e-05, ((0, 2), (2, 16)), jnp.float32),
        "mom_proj": gaussian(seeds[14], (LAYERS, D, D), (0.02 * (VOCAB * D + 24 * D * D) ** -0.5), 1.52587890625e-05, ((0, 2), (2, 16)), jnp.float32),
        "mom_fc": gaussian(seeds[15], (LAYERS, D, FF), (0.02 * (VOCAB * D + 24 * D * D) ** -0.5), 1.52587890625e-05, ((0, 2), (2, 16)), jnp.float32),
        "mom_down": gaussian(seeds[16], (LAYERS, D, FF), (0.02 * (VOCAB * D + 24 * D * D) ** -0.5), 1.52587890625e-05, ((0, 2), (2, 16)), jnp.float32),
        "layer_vecs": draw_layer_vecs(jax.random.fold_in(seeds[23], 71), 0),
        "vecs_m": gaussian(seeds[18], (LAYERS, 12, D), (0.555 * 0.02 * (VOCAB * D + 24 * D * D) ** -0.5), 9.5367431640625e-06, ((0, 2), (2, 16)), jnp.float32),
        "vecs_v": jnp.clip(jnp.exp(math.log(3.985660065874974e-11) - 1.3862944 * jax.random.uniform(seeds[19], (LAYERS, 12, D), jnp.float32) ** steps_of(seeds[19], (LAYERS, 12, D), ((0, 2), (2, 16)), -0.2, 0.2)), 9.964150164687435e-12, 3.985660065874974e-11),
        "final_norm": draw_final_norm(jax.random.fold_in(seeds[23], 71), 0),
        "norm_m": gaussian(seeds[21], (2, D), (0.555 * 0.02 * (VOCAB * D + 24 * D * D) ** -0.5), 9.5367431640625e-06, ((1, 16),), jnp.float32),
        "norm_v": jnp.clip(jnp.exp(math.log(3.985660065874974e-11) - 1.3862944 * jax.random.uniform(seeds[22], (2, D), jnp.float32) ** steps_of(seeds[22], (2, D), ((1, 16),), -0.2, 0.2)), 9.964150164687435e-12, 3.985660065874974e-11),
    }


LN_EPS = 1e-05
NEG_FILL = -1e+30
Z_WEIGHT = 0.01
CLIP_NORM = 0.02
MOMENTUM = 0.5
MUON_RATE = 0.7
MUON_DECAY = 0.01
ADAM_ONE = 0.9
ADAM_TWO = 0.95
ADAM_EPS = 1e-08
ADAM_DECAY = 0.1
RATE_EMBED = 0.12
RATE_POS = 0.1
RATE_VEC = 0.2
NEWTON_COEFS = (3.4445, -4.775, 2.0315)
PRECISE = lax.Precision.HIGHEST

@jax.custom_vjp
def low(v):
    return lax.optimization_barrier(v.astype(jnp.bfloat16)).astype(jnp.float32)

@jax.custom_vjp
def low_back(v):
    return v

def low_keep(v):
    return (low(v), None)

def low_pass(kept, grad):
    return (grad,)

def back_keep(v):
    return (v, None)

def back_low(kept, grad):
    return (low(grad),)
low.defvjp(low_keep, low_pass)
low_back.defvjp(back_keep, back_low)

def layer_norm(values, gain_row, bias_row):
    average = lax.optimization_barrier(jnp.mean(values, -1, keepdims=True))
    centered = values - average
    variance = lax.optimization_barrier(jnp.mean(centered * centered, -1, keepdims=True))
    return centered * lax.rsqrt(variance + LN_EPS) * gain_row + bias_row

def split_vectors(vectors):
    return (vectors[0], vectors[1], vectors[2], vectors[3], vectors[4], vectors[5], vectors[6], vectors[7:11].reshape(-1), vectors[11])

def matmul(left_mat, right_mat):
    return jnp.matmul(left_mat, right_mat, precision=PRECISE)

def layer_apply(inputs, w_qkv, w_proj, w_fc, w_down, vectors):
    batch_size, seq_len, model_width = inputs.shape
    head_count = model_width // HD
    factor = HD ** (-0.5)
    g_one, b_one, q_bias, v_bias, p_bias, g_two, b_two, f_bias, d_bias = split_vectors(vectors)
    normed_a = low(layer_norm(inputs, g_one, b_one))
    bias_qkv = jnp.concatenate([q_bias, jnp.zeros_like(q_bias), v_bias])
    qkv_rows = low(low_back(matmul(normed_a, w_qkv) + bias_qkv))
    queries = qkv_rows[..., :model_width].reshape(batch_size, seq_len, head_count, HD)
    keys_all = qkv_rows[..., model_width:2 * model_width].reshape(batch_size, seq_len, head_count, HD)
    values_all = qkv_rows[..., 2 * model_width:].reshape(batch_size, seq_len, head_count, HD)
    scores = jnp.einsum('bqhd,bkhd->bhqk', queries, keys_all, precision=PRECISE) * factor
    causal = jnp.tril(jnp.ones((seq_len, seq_len), bool))
    scores = low_back(jnp.where(causal, scores, NEG_FILL))
    attn_probs = jax.nn.softmax(scores, axis=-1)
    attended = jnp.einsum('bhqk,bkhd->bqhd', low(attn_probs), values_all, precision=PRECISE)
    attended = low(low_back(attended.reshape(batch_size, seq_len, model_width)))
    after_attn = inputs + low_back(matmul(attended, w_proj) + p_bias)
    normed_b = low(layer_norm(after_attn, g_two, b_two))
    hidden_pre = low_back(matmul(normed_b, w_fc) + f_bias)
    hidden_low = low(jax.nn.gelu(hidden_pre, approximate=True))
    return after_attn + low_back(matmul(hidden_low, w_down.T) + d_bias)

def adam_step(weights_in, gradient, first_mom, second_mom, step_rate):
    first_new = ADAM_ONE * first_mom + (1.0 - ADAM_ONE) * gradient
    second_new = ADAM_TWO * second_mom + (1.0 - ADAM_TWO) * gradient * gradient
    first_hat = first_new / (1.0 - ADAM_ONE ** STEP)
    second_hat = second_new / (1.0 - ADAM_TWO ** STEP)
    weights_new = weights_in - step_rate * (first_hat / (jnp.sqrt(second_hat) + ADAM_EPS) + ADAM_DECAY * weights_in)
    return (weights_new, first_new, second_new)

def orthogonalize(matrix):
    gram_full = matmul(matrix, matrix.T)
    inverse = 1.0 / (jnp.sqrt(jnp.trace(gram_full)) + 1e-07)
    iterate = matrix * inverse
    gram_full = gram_full * (inverse * inverse)
    for iteration in range(5):
        if iteration > 0:
            gram_full = matmul(iterate, iterate.T)
        once_applied = matmul(gram_full, iterate)
        twice_applied = matmul(gram_full, once_applied)
        iterate = NEWTON_COEFS[0] * iterate + NEWTON_COEFS[1] * once_applied + NEWTON_COEFS[2] * twice_applied
    return iterate

def reference(token_ids, target_ids, true_counts, embed_table, embed_m, embed_v, pos_table, pos_m, pos_v, w_qkv, w_proj, w_fc, w_down, mom_qkv, mom_proj, mom_fc, mom_down, layer_vecs, vecs_m, vecs_v, final_norm, norm_m, norm_v):
    places = jnp.arange(SEQ, dtype=jnp.int32)
    valid_mask = (places[None, None, :] < true_counts[:, :, None]).astype(jnp.float32)
    token_total = jnp.sum(true_counts).astype(jnp.float32)

    def objective(embed, pos, qkv, proj, fc, down, vecs, fnorm):
        table = low(embed)
        hidden = table[token_ids.reshape(-1, SEQ)] + low(pos)[None]
        for layer_num in range(LAYERS):
            hidden = layer_apply(hidden, low(qkv[layer_num]), low(proj[layer_num]), low(fc[layer_num]), low(down[layer_num]), low(vecs[layer_num]))
        norm_low = low(fnorm)
        normed = low(layer_norm(hidden, norm_low[0], norm_low[1])).reshape(-1, D)
        targets = target_ids.reshape(-1)
        counted = valid_mask.reshape(-1)
        row_count = normed.shape[0]
        block_rows = min(1024, row_count)

        def head_block(block_idx):
            start = block_idx * block_rows
            row_block = lax.dynamic_slice_in_dim(normed, start, block_rows, 0)
            target_block = lax.dynamic_slice_in_dim(targets, start, block_rows, 0)
            count_block = lax.dynamic_slice_in_dim(counted, start, block_rows, 0)
            logits = low_back(matmul(row_block, table.T))
            partition = jax.nn.logsumexp(logits, axis=-1)
            target_logit = jnp.take_along_axis(logits, target_block[:, None], axis=1)[:, 0]
            return jnp.sum(count_block * (partition - target_logit + Z_WEIGHT * partition * partition))
        loss_terms = lax.map(jax.checkpoint(head_block), jnp.arange(row_count // block_rows, dtype=jnp.int32))
        loss_total = jnp.sum(loss_terms)
        return (loss_total / token_total, loss_total)
    loss_value, pull, loss_sum = jax.vjp(objective, embed_table, pos_table, w_qkv, w_proj, w_fc, w_down, layer_vecs, final_norm, has_aux=True)
    grads = pull(jnp.ones_like(loss_value))
    clip_norm = jnp.sqrt(sum((jnp.sum(gradient * gradient) for gradient in grads)))
    factor = jnp.minimum(1.0, CLIP_NORM / (clip_norm + 1e-06))
    grads = [gradient * factor for gradient in grads]
    embed_new, embed_m_new, embed_v_new = adam_step(embed_table, grads[0], embed_m, embed_v, RATE_EMBED)
    pos_new, pos_m_new, pos_v_new = adam_step(pos_table, grads[1], pos_m, pos_v, RATE_POS)
    vecs_new, vecs_m_new, vecs_v_new = adam_step(layer_vecs, grads[6], vecs_m, vecs_v, RATE_VEC)
    norm_new, norm_m_new, norm_v_new = adam_step(final_norm, grads[7], norm_m, norm_v, RATE_VEC)
    results = []
    for master, moment, gradient in ((w_qkv, mom_qkv, grads[2]), (w_proj, mom_proj, grads[3]), (w_fc, mom_fc, grads[4]), (w_down, mom_down, grads[5])):
        new_list = []
        mom_list = []
        for layer_num in range(LAYERS):
            mom_next = MOMENTUM * moment[layer_num] + gradient[layer_num]
            ortho = orthogonalize(mom_next)
            column_factor = math.sqrt(master.shape[2] / master.shape[1])
            new_list.append(master[layer_num] - MUON_RATE * (column_factor * ortho + MUON_DECAY * master[layer_num]))
            mom_list.append(mom_next)
        new_stack = jnp.stack(new_list)
        results.append((new_stack, new_stack.astype(jnp.bfloat16), jnp.stack(mom_list)))
    return (loss_sum, clip_norm, embed_new, embed_new.astype(jnp.bfloat16), embed_m_new, embed_v_new, pos_new, pos_m_new, pos_v_new, results[0][0], results[0][1], results[0][2], results[1][0], results[1][1], results[1][2], results[2][0], results[2][1], results[2][2], results[3][0], results[3][1], results[3][2], vecs_new, vecs_m_new, vecs_v_new, norm_new, norm_m_new, norm_v_new)
```

```python
import functools
import math

import jax
import jax.numpy as jnp
from jax import lax
from jax.experimental import pallas as pl
from jax.experimental.pallas import tpu as pltpu
from jax.sharding import Mesh
from jax.sharding import PartitionSpec as P

HD = 64
STEP = 10


LN_EPS = 1e-05
NEG_FILL = -1e30
Z_WEIGHT = 0.01
CLIP_NORM = 0.02
MOMENTUM = 0.5
MUON_RATE = 0.7
MUON_DECAY = 0.01
ADAM_ONE = 0.9
ADAM_TWO = 0.95
ADAM_EPS = 1e-08
ADAM_DECAY = 0.1
RATE_EMBED = 0.12
RATE_POS = 0.1
RATE_VEC = 0.2
NEWTON_COEFS = (3.4445, -4.775, 2.0315)
FSDP = ("za", "yb", "yc", "xd")
SPOTS = ("za", "yb")
GROUP = ("section", "yc", "xd")
NOTE = 8
UPPER = ((0, 0), (0, 1), (0, 2), (1, 1), (1, 2), (2, 2))
MOMENT_SCALE = 2.0**21
VMEM_BYTES = 56 * 1024 * 1024


def swapped(block, axis):
    size = lax.axis_size(axis)
    return lax.ppermute(block, axis, [(i, size - 1 - i) for i in range(size)])


def spread_small(block):
    count = lax.axis_size(FSDP)
    copies = jnp.broadcast_to(block[None], (count,) + block.shape)
    return lax.all_to_all(copies, FSDP, 0, 0, tiled=True)


def span():
    return (lax.axis_size("za"), lax.axis_size(("yb", "yc")), lax.axis_size("xd"))


def route(level, distance):
    za, yb, xd = span()
    pairs = []
    for section in range(2):
        for place in range(za * yb * xd):
            a, b, c = place // (yb * xd), place // xd % yb, place % xd
            if level == 2:
                a = (a + distance) % za
            elif section == level:
                b = (b + distance) % yb
            else:
                c = (c + distance) % xd
            start = section * za * yb * xd
            pairs.append((start + place, start + (a * yb + b) * xd + c))
    return pairs


def moved(block, level, distance=1):
    return lax.ppermute(block, ("section",) + FSDP, route(level, distance))


def pick(block, axis, index):
    return lax.dynamic_index_in_dim(block, index, axis, keepdims=False)


def after(value, *others):
    return lax.optimization_barrier((value,) + others)[0]


def column_near(block):
    return jnp.stack([block] + [moved(block, 2, -k) for k in range(1, span()[0])])


def plane_near(column):
    return jnp.stack([column] + [moved(column, 1, -k) for k in range(1, span()[2])])


def planes_near(plane):
    return [plane] + [moved(plane, 0, -k) for k in range(1, span()[1])]


def gathered_near(block):
    return planes_near(plane_near(column_near(block)))


def owners_near(section):
    za, yb, xd = span()
    a, b, c = lax.axis_index("za"), lax.axis_index(("yb", "yc")), lax.axis_index("xd")
    places = jnp.arange(za * yb * xd, dtype=jnp.int32)
    far, near, high = places // (xd * za), places // za % xd, places % za
    high = (a + high) % za
    row = jnp.where(section == 0, (b + far) % yb, (b + near) % yb)
    col = jnp.where(section == 0, (c + near) % xd, (c + far) % xd)
    return (high * yb + row) * xd + col


def places_near(section):
    za, yb, xd = span()
    a, b, c = lax.axis_index("za"), lax.axis_index(("yb", "yc")), lax.axis_index("xd")
    owners = jnp.arange(za * yb * xd, dtype=jnp.int32)
    high = (owners // (yb * xd) - a) % za
    row, col = (owners // xd % yb - b) % yb, (owners % xd - c) % xd
    far, near = jnp.where(section == 0, row, col), jnp.where(section == 0, col, row)
    return (far * xd + near) * za + high


def assemble_kernel(widths, each, spot_ref, *refs):
    sources, outs = refs[: -len(widths)], refs[-len(widths) :]
    for number, source in enumerate(sources):

        @pl.when(pl.program_id(0) // each == number)
        def _(source=source):
            start = 0
            for out, width in zip(outs, widths):
                out[...] = source[0, start : start + width, :]
                start += width


def assembled(own, other, widths):
    section = lax.axis_index("section")
    count = lax.axis_size(FSDP)
    rows, half = own[0].shape[-2:]
    pieces = [piece.reshape(-1, rows, half) for piece in own + other]
    if any(width % 16 for width in widths):
        sides = []
        for side, parts in ((section, pieces[: len(own)]), (1 - section, pieces[len(own) :])):
            sides.append(jnp.take(jnp.concatenate(parts), places_near(side), axis=0))
        first_side = section == 0
        left = jnp.where(first_side, sides[0], sides[1])
        right = jnp.where(first_side, sides[1], sides[0])
        whole = jnp.concatenate([left, right], -1)
        starts = [sum(widths[:n]) for n in range(5)]
        return [whole[:, starts[n] : starts[n + 1]].reshape(-1, 2 * half) for n in range(4)]
    sides = jnp.stack([section, 1 - section]).astype(jnp.int32)
    spots = jnp.concatenate(
        [owners_near(section), owners_near(1 - section), jnp.repeat(sides, count)]
    ).astype(jnp.int32)
    each = pieces[0].shape[0]

    def source_at(number):
        return lambda step, spot: (jnp.clip(step - number * each, 0, each - 1), 0, 0)

    return pl.pallas_call(
        functools.partial(assemble_kernel, tuple(widths), each),
        grid_spec=pltpu.PrefetchScalarGridSpec(
            num_scalar_prefetch=1,
            grid=(2 * count,),
            in_specs=[
                pl.BlockSpec((1, rows, half), source_at(number)) for number in range(len(pieces))
            ],
            out_specs=[
                pl.BlockSpec((width, half), lambda step, spot: (spot[step], spot[2 * count + step]))
                for width in widths
            ],
        ),
        out_shape=[
            jax.ShapeDtypeStruct((count * width, 2 * half), jnp.bfloat16) for width in widths
        ],
        compiler_params=pltpu.CompilerParams(vmem_limit_bytes=VMEM_BYTES),
        cost_estimate=pl.CostEstimate(
            flops=0, bytes_accessed=8 * count * rows * half, transcendentals=0
        ),
    )(spots, *pieces)


def exponent_for(bound):
    return jnp.floor(14.5 - jnp.log2(jnp.maximum(bound, 1e-30)))


def coded(values, exponent):
    rows = lax.broadcasted_iota(jnp.int32, values.shape, values.ndim - 2)
    noted = rows >= values.shape[-2] - NOTE
    return jnp.where(noted, exponent, values * jnp.exp2(exponent)).astype(jnp.float16)


def exponent_in(block):
    return block[(0,) * (block.ndim - 2) + (block.shape[-2] - 1, 0)].astype(jnp.float32)


def added(kept, came):
    first, second = exponent_in(kept), exponent_in(came)
    total = kept.astype(jnp.float32) * jnp.exp2(-first) + came.astype(jnp.float32) * jnp.exp2(
        -second
    )
    return coded(total, jnp.minimum(first, second) - 1.0)


def planes_cut(block):
    first_side = lax.axis_index("section") == 0
    sizes = span()
    block = block.reshape(sizes + block.shape[1:])
    b, c = lax.axis_index(("yb", "yc")), lax.axis_index("xd")
    parts = []
    for distance in range(sizes[1]):
        row, col = (b + distance) % sizes[1], (c + distance) % sizes[2]
        parts.append(jnp.where(first_side, pick(block, 1, row), pick(block, 2, col)))
    return parts


def planes_reduced(parts, add):
    total = parts[0]
    for distance in range(1, len(parts)):
        total = add(total, moved(parts[distance], 0, distance))
    return total


def plane_reduced(plane, add):
    first_side = lax.axis_index("section") == 0
    inner = jnp.where(first_side, lax.axis_index("xd"), lax.axis_index(("yb", "yc")))
    total = pick(plane, 1, inner)
    for distance in range(1, span()[2]):
        sent = pick(plane, 1, (inner + distance) % span()[2])
        total = add(total, moved(sent, 1, distance))
    return total


def column_parts(column):
    a = lax.axis_index("za")
    parts = [pick(column, 0, a)]
    for distance in range(1, span()[0]):
        parts.append(moved(pick(column, 0, (a + distance) % span()[0]), 2, distance))
    return parts


def decoded(block):
    return block[..., :-NOTE, :].astype(jnp.float32) * jnp.exp2(-exponent_in(block))


def row_sums(block):
    plane = planes_reduced(planes_cut(block), lax.add)
    return sum(part.astype(jnp.float32) for part in column_parts(plane_reduced(plane, lax.add)))


def parted_weights(grads, exponent):
    own = [grad.reshape(lax.axis_size(FSDP), -1, grad.shape[-1]) for grad in grads]
    note = jnp.broadcast_to(exponent.astype(jnp.float16), (own[0].shape[0], NOTE, own[0].shape[2]))
    return planes_cut(jnp.concatenate(own + [note], 1))


def summed_weights(layer_parts, *before):
    first_side = lax.axis_index("section") == 0
    plane_late = planes_reduced(layer_parts[1], added)
    column_late = plane_reduced(plane_late, added)
    parts_early = [after(part, column_late) for part in layer_parts[0]]
    plane_early = planes_reduced(parts_early, added)
    parts_late = column_parts(column_late)
    column_early = plane_reduced(plane_early, added)
    parts_early = column_parts(column_early)
    parts_early[0] = after(parts_early[0], *before)
    halves = [sum(decoded(part) for part in parts) for parts in (parts_early, parts_late)]
    kept = jnp.where(first_side, halves[0], halves[1])
    came = swapped(jnp.where(first_side, halves[1], halves[0]), "section")
    return jnp.where(
        first_side, jnp.concatenate([kept, came], 1), jnp.concatenate([came, kept], 1)
    )


def gram_summed(gram):
    tile = gram.shape[0] // 3
    blocks = [gram[i * tile : (i + 1) * tile, j * tile : (j + 1) * tile] for i, j in UPPER]
    near, far = jnp.stack(blocks[:3]), jnp.stack(blocks[3:])
    if lax.axis_size(GROUP) != 4:
        return lax.psum(jnp.concatenate([near, far]), GROUP)
    first_side = lax.axis_index("section") == 0
    kept, gone = jnp.where(first_side, near, far), jnp.where(first_side, far, near)
    kept = kept + swapped(gone, "section")
    kept = kept + swapped(kept, "xd")
    came = swapped(kept, "section")
    return jnp.where(first_side, jnp.concatenate([kept, came]), jnp.concatenate([came, kept]))


def layer_norm(values, gain_row, bias_row):
    average = jnp.mean(values, -1, keepdims=True)
    centered = values - average
    variance = jnp.mean(centered * centered, -1, keepdims=True)
    return centered * lax.rsqrt(variance + LN_EPS) * gain_row + bias_row


def split_vectors(vectors):
    rows = [vectors[number : number + 1] for number in range(12)]
    return (*rows[:7], jnp.concatenate(rows[7:11], 1), rows[11])


def contract_rows(left_mat, right_mat):
    return lax.dot_general(
        left_mat, right_mat, (((0,), (0,)), ((), ())), preferred_element_type=jnp.float32
    )


def contract_cols(left_mat, right_mat):
    return lax.dot_general(
        left_mat, right_mat, (((1,), (1,)), ((), ())), preferred_element_type=jnp.float32
    )


def plain_dot(left_mat, right_mat):
    return jnp.dot(left_mat, right_mat, preferred_element_type=jnp.float32)


def with_other(*values):
    joined = jnp.concatenate(values, 1)
    return jnp.concatenate([joined, swapped(joined, "section")], 0)


def own_half(values):
    half = values.shape[1] // 2
    return lax.dynamic_slice_in_dim(values, lax.axis_index("section") * half, half, 1)


def other_half(values):
    half = values.shape[1] // 2
    return lax.dynamic_slice_in_dim(values, (1 - lax.axis_index("section")) * half, half, 1)


def widest_column(values):
    return jnp.max(jnp.sum(jnp.square(values.astype(jnp.float32)), 0))


def gelu_tanh(values):
    return jax.nn.gelu(values, approximate=True)


def layer_forward(inputs, weights):
    qkv_t, proj_t, fc_t, down_t, vectors = weights
    g_one, b_one, q_bias, v_bias, p_bias, g_two, b_two, f_bias, d_bias = split_vectors(vectors)
    seq_len, model_width = inputs.shape
    head_count = model_width // HD
    factor = HD ** (-0.5)
    normed_a = layer_norm(inputs, g_one, b_one).astype(jnp.bfloat16)
    bias_qkv = jnp.concatenate([q_bias, jnp.zeros_like(q_bias), v_bias], 1)
    qkv_rows = (contract_cols(normed_a, qkv_t) + bias_qkv).astype(jnp.bfloat16)
    queries = qkv_rows[:, :model_width].reshape(seq_len, head_count, HD)
    keys_all = qkv_rows[:, model_width : 2 * model_width].reshape(seq_len, head_count, HD)
    values_all = qkv_rows[:, 2 * model_width :].reshape(seq_len, head_count, HD)
    scores = (
        jnp.einsum("qhd,khd->hqk", queries, keys_all, preferred_element_type=jnp.float32) * factor
    )
    causal = lax.broadcasted_iota(jnp.int32, (seq_len, seq_len), 0) >= lax.broadcasted_iota(
        jnp.int32, (seq_len, seq_len), 1
    )
    attn_probs = jax.nn.softmax(jnp.where(causal, scores, NEG_FILL), axis=-1)
    probs_low = attn_probs.astype(jnp.bfloat16)
    attended = jnp.einsum("hqk,khd->qhd", probs_low, values_all, preferred_element_type=jnp.float32)
    attended = attended.reshape(seq_len, model_width).astype(jnp.bfloat16)
    after_attn = inputs + contract_cols(attended, proj_t) + p_bias
    normed_b = layer_norm(after_attn, g_two, b_two).astype(jnp.bfloat16)
    hidden_pre = contract_cols(normed_b, fc_t) + f_bias
    hidden_low = gelu_tanh(hidden_pre).astype(jnp.bfloat16)
    outputs = after_attn + plain_dot(hidden_low, down_t) + d_bias
    saved = (
        inputs,
        normed_a,
        queries,
        keys_all,
        values_all,
        attn_probs,
        probs_low,
        attended,
        after_attn,
        normed_b,
        hidden_pre,
        with_other(hidden_low, normed_a, attended, normed_b),
    )
    return (outputs, saved)


def layer_backward(saved, grad_out, weights):
    qkv_t, proj_t, fc_t, down_t, vectors = weights
    g_one, b_one, q_bias, v_bias, p_bias, g_two, b_two, f_bias, d_bias = split_vectors(vectors)
    (
        inputs,
        normed_a,
        queries,
        keys_all,
        values_all,
        attn_probs,
        probs_low,
        attended,
        after_attn,
        normed_b,
        hidden_pre,
        early,
    ) = saved
    seq_len, model_width = inputs.shape
    factor = HD ** (-0.5)
    grad_mlp = grad_out.astype(jnp.bfloat16)
    d_dbias = jnp.sum(grad_mlp, 0, keepdims=True, dtype=jnp.float32)
    grad_hidden = contract_cols(grad_mlp, down_t)
    grad_pre = jax.vjp(gelu_tanh, hidden_pre)[1](grad_hidden)[0].astype(jnp.bfloat16)
    d_fbias = jnp.sum(grad_pre, 0, keepdims=True, dtype=jnp.float32)
    grad_nb = plain_dot(grad_pre, fc_t)
    ln_two = jax.vjp(layer_norm, after_attn, g_two, b_two)[1](grad_nb)
    grad_mid = grad_out + ln_two[0]
    grad_attn = grad_mid.astype(jnp.bfloat16)
    d_pbias = jnp.sum(grad_attn, 0, keepdims=True, dtype=jnp.float32)
    grad_att = plain_dot(grad_attn, proj_t).reshape(queries.shape).astype(jnp.bfloat16)
    grad_probs = jnp.einsum(
        "qhd,khd->hqk", grad_att, values_all, preferred_element_type=jnp.float32
    )
    grad_vals = jnp.einsum("hqk,qhd->khd", probs_low, grad_att, preferred_element_type=jnp.float32)
    grad_scores = attn_probs * (grad_probs - jnp.sum(grad_probs * attn_probs, -1, keepdims=True))
    grad_scores = grad_scores.astype(jnp.bfloat16)
    grad_q = (
        jnp.einsum("hqk,khd->qhd", grad_scores, keys_all, preferred_element_type=jnp.float32)
        * factor
    )
    grad_k = (
        jnp.einsum("hqk,qhd->khd", grad_scores, queries, preferred_element_type=jnp.float32)
        * factor
    )
    grad_qkv = jnp.concatenate(
        [
            grad_q.reshape(seq_len, model_width),
            grad_k.reshape(seq_len, model_width),
            grad_vals.reshape(seq_len, model_width),
        ],
        -1,
    ).astype(jnp.bfloat16)
    qkv_sums = jnp.sum(grad_qkv, 0, keepdims=True, dtype=jnp.float32)
    late = with_other(grad_qkv, grad_attn, grad_pre, grad_mlp)
    wide = hidden_pre.shape[1]

    def taken(block, start, width):
        return block[:, start : start + width]

    products = (
        (taken(late, 0, 3 * model_width), taken(early, wide, model_width)),
        (taken(late, 3 * model_width, model_width), taken(early, wide + model_width, model_width)),
        (taken(late, 4 * model_width, wide), taken(early, wide + 2 * model_width, model_width)),
        (taken(early, 0, wide), taken(late, 4 * model_width + wide, model_width)),
    )
    bounds = [widest_column(block) for block in (early, late)]
    exponent = exponent_for(jnp.sqrt(bounds[0]) * jnp.sqrt(bounds[1]))
    scale = jnp.exp2(exponent)
    d_qkv, d_proj, d_fc, d_down = (
        (contract_rows(left, own_half(right)) * scale).astype(jnp.float16)
        for left, right in products
    )
    grad_na = plain_dot(grad_qkv, qkv_t)
    ln_one = jax.vjp(layer_norm, inputs, g_one, b_one)[1](grad_na)
    grad_in = grad_mid + ln_one[0]
    d_vectors = [
        ln_one[1],
        ln_one[2],
        qkv_sums[:, :model_width],
        qkv_sums[:, 2 * model_width :],
        d_pbias,
        ln_two[1],
        ln_two[2],
        *(d_fbias[:, n * model_width : (n + 1) * model_width] for n in range(4)),
        d_dbias,
    ]
    return (grad_in, (d_qkv, d_proj, d_fc, d_down), d_vectors, exponent)


def adam_step(weights_in, gradient, first_mom, second_mom, step_rate):
    first_new = ADAM_ONE * first_mom + (1.0 - ADAM_ONE) * gradient
    second_new = ADAM_TWO * second_mom + (1.0 - ADAM_TWO) * gradient * gradient
    first_hat = first_new / (1.0 - ADAM_ONE**STEP)
    second_hat = second_new / (1.0 - ADAM_TWO**STEP)
    weights_new = weights_in - step_rate * (
        first_hat / (jnp.sqrt(second_hat) + ADAM_EPS) + ADAM_DECAY * weights_in
    )
    return (weights_new, first_new, second_new)


def halves_of(values):
    high = values.astype(jnp.bfloat16)
    return (high, (values - high.astype(jnp.float32)).astype(jnp.bfloat16))


def newton_kernel(gram_ref, out_ref, pair_a, pair_b, gram_now, poly, product):
    tile = gram_ref.shape[1]
    count = 3
    width = count * tile
    a, b, c = NEWTON_COEFS
    rows = lax.broadcasted_iota(jnp.int32, (width, width), 0)
    cols = lax.broadcasted_iota(jnp.int32, (width, width), 1)
    diagonal = rows == cols

    def store_pair(pair, values):
        for part in range(3):
            pair[part] = values.astype(jnp.bfloat16)
            values = values - pair[part].astype(jnp.float32)

    def multiply(left, right, write, terms=2):
        for i in range(count):
            row_at = slice(i * tile, (i + 1) * tile)
            for j in range(i, count):
                col_at = slice(j * tile, (j + 1) * tile)
                block = jnp.zeros((tile, tile), jnp.float32)
                for part in reversed(range(terms)):
                    for other in reversed(range(terms - part)):
                        block += plain_dot(left[part, row_at, :], right[other, :, col_at])
                write(row_at, col_at, block)
                if i != j:
                    write(col_at, row_at, block.T)

    def into(ref):
        def write(row_at, col_at, block):
            ref[row_at, col_at] = block

        return write

    for number, (i, j) in enumerate(UPPER):
        row_at, col_at = slice(i * tile, (i + 1) * tile), slice(j * tile, (j + 1) * tile)
        gram_now[row_at, col_at] = gram_ref[number]
        if i != j:
            gram_now[col_at, row_at] = gram_ref[number].T
    full = gram_now[...]
    trace = jnp.sum(jnp.where(diagonal, full, 0.0))
    inverse = 1.0 / (jnp.sqrt(jnp.full((1, 1), trace, jnp.float32)) + 1e-07)
    gram_now[...] = full * (inverse * inverse)
    for iteration in range(5):
        store_pair(pair_a, gram_now[...])
        multiply(pair_a, pair_a, into(poly))
        poly[...] = jnp.where(diagonal, a, 0.0) + b * gram_now[...] + c * poly[...]
        store_pair(pair_b, poly[...])
        if iteration < 4:
            terms = 3 if iteration < 2 else 2
            multiply(pair_a, pair_b, into(gram_now), terms)
            store_pair(pair_a, gram_now[...])
            multiply(pair_a, pair_b, into(gram_now), terms)
        if iteration == 0:
            product[...] = poly[...]
        else:
            store_pair(pair_a, product[...])
            multiply(pair_a, pair_b, into(product))
    out_ref[...] = product[...] * inverse


def newton_product(gram_blocks):
    width = 3 * gram_blocks.shape[1]
    square = (width, width)
    return pl.pallas_call(
        newton_kernel,
        out_shape=jax.ShapeDtypeStruct(square, jnp.float32),
        in_specs=[pl.BlockSpec(memory_space=pltpu.VMEM)],
        out_specs=pl.BlockSpec(memory_space=pltpu.VMEM),
        scratch_shapes=[
            pltpu.VMEM((3,) + square, jnp.bfloat16),
            pltpu.VMEM((3,) + square, jnp.bfloat16),
            pltpu.VMEM(square, jnp.float32),
            pltpu.VMEM(square, jnp.float32),
            pltpu.VMEM(square, jnp.float32),
        ],
        compiler_params=pltpu.CompilerParams(vmem_limit_bytes=48 * 1024 * 1024),
        cost_estimate=pl.CostEstimate(
            flops=17 * 4 * width**3, bytes_accessed=8 * width * width, transcendentals=0
        ),
    )(gram_blocks)


def head_forward_kernel(
    shard_rows, spot_ref, one_ref, two_ref, table_ref, target_ref, exp_ref, stat_ref, row_ref
):
    rows = jnp.concatenate([one_ref[0], two_ref[0]], 0)
    row_ref[...] = rows
    logits = contract_cols(rows, table_ref[...])
    cols = lax.broadcasted_iota(jnp.int32, logits.shape, 1)
    logits = jnp.where(cols < shard_rows, logits, NEG_FILL)
    highest = jnp.max(logits, -1, keepdims=True)
    exps = jnp.exp(logits - highest)
    total = jnp.sum(exps, -1, keepdims=True)
    target = jnp.sum(jnp.where(cols == target_ref[...], logits, 0.0), -1, keepdims=True)
    exp_ref[...] = exps.astype(jnp.bfloat16)
    lanes = lax.broadcasted_iota(jnp.int32, stat_ref.shape, 1)
    stat_ref[...] = jnp.where(lanes == 0, highest, jnp.where(lanes == 1, total, target))


def head_forward(blocks, places, table, targets, shard_rows):
    number, tokens, width = blocks.shape
    count = number * tokens
    vocab = table.shape[0]
    step = 2 * tokens
    return pl.pallas_call(
        functools.partial(head_forward_kernel, shard_rows),
        grid_spec=pltpu.PrefetchScalarGridSpec(
            num_scalar_prefetch=1,
            grid=(number // 2,),
            in_specs=[
                pl.BlockSpec((1, tokens, width), lambda i, spot: (spot[2 * i], 0, 0)),
                pl.BlockSpec((1, tokens, width), lambda i, spot: (spot[2 * i + 1], 0, 0)),
                pl.BlockSpec((vocab, width), lambda i, spot: (0, 0)),
                pl.BlockSpec((step, 1), lambda i, spot: (i, 0)),
            ],
            out_specs=[
                pl.BlockSpec((step, vocab), lambda i, spot: (i, 0)),
                pl.BlockSpec((step, 128), lambda i, spot: (i, 0)),
                pl.BlockSpec((step, width), lambda i, spot: (i, 0)),
            ],
        ),
        out_shape=[
            jax.ShapeDtypeStruct((count, vocab), jnp.bfloat16),
            jax.ShapeDtypeStruct((count, 128), jnp.float32),
            jax.ShapeDtypeStruct((count, width), jnp.bfloat16),
        ],
        compiler_params=pltpu.CompilerParams(vmem_limit_bytes=VMEM_BYTES),
        cost_estimate=pl.CostEstimate(
            flops=2 * count * vocab * width,
            bytes_accessed=2 * (vocab * width + count * (width + vocab)),
            transcendentals=count * vocab,
        ),
    )(places, blocks, blocks, table, targets)


def head_pull_kernel(exp_ref, target_ref, table_ref, soft_ref, hard_ref):
    exps = exp_ref[...]
    cols = lax.broadcasted_iota(jnp.int32, exps.shape, 1)
    chosen = jnp.where(cols == target_ref[...], 1.0, 0.0).astype(jnp.bfloat16)
    soft_ref[...] = plain_dot(exps, table_ref[...])
    hard_ref[...] = plain_dot(chosen, table_ref[...]).astype(jnp.bfloat16)


def head_pull(exps, targets, table):
    count, vocab = exps.shape
    width = table.shape[1]
    step = min(256, count)
    return pl.pallas_call(
        head_pull_kernel,
        grid=(count // step,),
        out_shape=[
            jax.ShapeDtypeStruct((count, width), jnp.float32),
            jax.ShapeDtypeStruct((count, width), jnp.bfloat16),
        ],
        in_specs=[
            pl.BlockSpec((step, vocab), lambda i: (i, 0)),
            pl.BlockSpec((step, 1), lambda i: (i, 0)),
            pl.BlockSpec((vocab, width), lambda i: (0, 0)),
        ],
        out_specs=[
            pl.BlockSpec((step, width), lambda i: (i, 0)),
            pl.BlockSpec((step, width), lambda i: (i, 0)),
        ],
        compiler_params=pltpu.CompilerParams(vmem_limit_bytes=VMEM_BYTES),
        cost_estimate=pl.CostEstimate(
            flops=4 * count * vocab * width,
            bytes_accessed=2 * (vocab * width + count * (3 * width + vocab)),
            transcendentals=0,
        ),
    )(exps, targets, table)


def head_table_kernel(exp_ref, token_ref, target_ref, row_ref, grad_ref):
    exps = exp_ref[...].astype(jnp.float32)
    cols = lax.broadcasted_iota(jnp.int32, exps.shape, 1)
    at_target = jnp.where(cols == target_ref[...], token_ref[:, 1:2], 0.0)
    grad_logit = (exps * token_ref[:, 0:1] - at_target).astype(jnp.bfloat16)

    @pl.when(pl.program_id(0) == 0)
    def _():
        grad_ref[...] = jnp.zeros_like(grad_ref)

    grad_ref[...] += contract_rows(grad_logit, row_ref[...])


def head_table(exps, token_scales, targets, rows):
    count, vocab = exps.shape
    width = rows.shape[1]
    step = min(256, count)
    return pl.pallas_call(
        head_table_kernel,
        grid=(count // step,),
        out_shape=jax.ShapeDtypeStruct((vocab, width), jnp.float32),
        in_specs=[
            pl.BlockSpec((step, vocab), lambda i: (i, 0)),
            pl.BlockSpec((step, 2), lambda i: (i, 0)),
            pl.BlockSpec((step, 1), lambda i: (i, 0)),
            pl.BlockSpec((step, width), lambda i: (i, 0)),
        ],
        out_specs=pl.BlockSpec((vocab, width), lambda i: (0, 0)),
        compiler_params=pltpu.CompilerParams(vmem_limit_bytes=VMEM_BYTES),
        cost_estimate=pl.CostEstimate(
            flops=2 * count * vocab * width,
            bytes_accessed=2 * (2 * vocab * width + count * (width + vocab)),
            transcendentals=0,
        ),
    )(exps, token_scales, targets, rows)


def row_scatter_kernel(id_ref, part_ref, total_ref, out_ref):
    @pl.when(pl.program_id(0) == 0)
    def _():
        out_ref[...] = total_ref[...]

    spots = lax.broadcasted_iota(jnp.int32, (out_ref.shape[0], id_ref.shape[1]), 0)
    chosen = jnp.where(spots == id_ref[...], 1.0, 0.0).astype(jnp.bfloat16)
    out_ref[...] += plain_dot(chosen, part_ref[...])


def rows_scattered(total, ids, parts):
    vocab, width = total.shape
    count = parts.shape[0]
    step = min(256, count)
    return pl.pallas_call(
        row_scatter_kernel,
        grid=(count // step,),
        out_shape=jax.ShapeDtypeStruct(total.shape, total.dtype),
        in_specs=[
            pl.BlockSpec((1, step), lambda i: (0, i)),
            pl.BlockSpec((step, width), lambda i: (i, 0)),
            pl.BlockSpec((vocab, width), lambda i: (0, 0)),
        ],
        out_specs=pl.BlockSpec((vocab, width), lambda i: (0, 0)),
        compiler_params=pltpu.CompilerParams(vmem_limit_bytes=VMEM_BYTES),
        cost_estimate=pl.CostEstimate(
            flops=2 * count * vocab * width,
            bytes_accessed=8 * vocab * width + 2 * count * width,
            transcendentals=0,
        ),
    )(ids.reshape(1, count), parts, total)


def shards(
    token_ids,
    target_ids,
    true_counts,
    embed_table,
    embed_m,
    embed_v,
    pos_table,
    pos_m,
    pos_v,
    w_qkv,
    w_proj,
    w_fc,
    w_down,
    mom_qkv,
    mom_proj,
    mom_fc,
    mom_down,
    layer_vecs,
    vecs_m,
    vecs_v,
    final_norm,
    norm_m,
    norm_v,
):
    section_index = lax.axis_index("section")
    section_count = lax.axis_size("section")
    fsdp_count = lax.axis_size(FSDP)
    shard_rows, model_width = embed_table.shape
    vocab_start = lax.axis_index(FSDP) * shard_rows
    vocab_rows = -(-shard_rows // 128) * 128
    table_rows = jnp.pad(embed_table.astype(jnp.bfloat16), ((0, vocab_rows - shard_rows), (0, 0)))
    masters_t = [w[0].T for w in (w_qkv, w_proj, w_fc, w_down)]
    moments_t = [m[0].T for m in (mom_qkv, mom_proj, mom_fc, mom_down)]
    widths = [w.shape[0] for w in masters_t]
    starts = [sum(widths[:number]) for number in range(5)]
    layer_rows, place_rows = layer_vecs.shape[1], pos_table.shape[0]
    norm_at = section_count * layer_rows
    places_at = norm_at + final_norm.shape[0]
    small_rows = -(-(places_at + place_rows) // 16) * 16

    def padded_rows(parts):
        missing = small_rows - sum(part.shape[0] for part in parts)
        return jnp.concatenate(parts + [jnp.zeros((missing, parts[0].shape[1]), parts[0].dtype)], 0)

    vecs_both = lax.all_gather(layer_vecs[0].astype(jnp.bfloat16), "section", axis=0, tiled=True)
    token_row = jnp.concatenate([token_ids[0], target_ids[0]], 1)
    token_row = jnp.concatenate([token_row // 256, token_row % 256], 1)
    lanes = layer_vecs.shape[2]
    token_rows = -(-token_row.shape[1] // lanes)
    token_row = jnp.pad(token_row, ((0, 0), (0, token_rows * lanes - token_row.shape[1])))
    token_row = token_row.reshape(token_rows, lanes).astype(jnp.bfloat16)
    small = padded_rows([vecs_both, final_norm.astype(jnp.bfloat16), pos_table.astype(jnp.bfloat16)])
    small = spread_small(jnp.concatenate([small, token_row], 0))
    ids_parts = small[:, small_rows:].astype(jnp.int32).reshape(fsdp_count, -1)
    seq_len = token_ids.shape[2]
    ids_targets = 256 * ids_parts[:, : 2 * seq_len] + ids_parts[:, 2 * seq_len : 4 * seq_len]
    ids_all, targets_all = ids_targets[:, :seq_len], ids_targets[:, seq_len:]
    seq_count = ids_all.shape[0]
    small = jnp.moveaxis(small[:, :small_rows], 0, 1).reshape(small_rows, model_width)
    small = small.astype(jnp.float32)
    head_norm = small[norm_at:places_at]
    positions = small[places_at : places_at + place_rows]
    pack = jnp.concatenate(masters_t, 0).astype(jnp.bfloat16)
    first_side = section_index == 0
    kept_half = own_half(pack)
    came_half = swapped(other_half(pack), "section")
    blocks = [jnp.where(section_index == layer, kept_half, came_half) for layer in range(2)]
    column_early = column_near(blocks[0])
    column_late = column_near(after(blocks[1], column_early))
    planes = [planes_near(plane_near(column_early))]
    planes.append(planes_near(plane_near(after(column_late, planes[0][-1]))))
    layer_sets = []
    for layer, own in enumerate(planes):
        other = [swapped(piece, "section") for piece in own]
        layer_sets.append(
            list(assembled(own, other, widths))
            + [small[layer * layer_rows : (layer + 1) * layer_rows]]
        )

    local_ids = ids_all - vocab_start
    inside = (local_ids >= 0) & (local_ids < shard_rows)
    safe_ids = jnp.clip(local_ids, 0, shard_rows - 1)
    contrib = jnp.where(
        inside[..., None], jnp.take(table_rows, safe_ids, axis=0), jnp.zeros((), jnp.bfloat16)
    )
    rows_in = row_sums(contrib)

    current = rows_in + positions
    kept = []
    for weights in layer_sets:
        current, saved = layer_forward(current, weights)
        kept.append(saved)
    final_rows = current
    normed_low = layer_norm(final_rows, head_norm[0:1], head_norm[1:2]).astype(jnp.bfloat16)
    blocks = jnp.concatenate(gathered_near(normed_low), 0).reshape((fsdp_count,) + normed_low.shape)
    counts_row = jnp.take(true_counts, section_index, axis=0)
    counted = lax.broadcasted_iota(jnp.int32, (seq_count, seq_len), 1) < counts_row[:, None]
    counted = counted.astype(jnp.float32).reshape(-1)
    token_total = jnp.sum(true_counts).astype(jnp.float32)
    local_targets = targets_all.reshape(-1) - vocab_start
    targets_col = jnp.where(local_targets < shard_rows, local_targets, -1)[:, None]
    exps, stats, rows_all = head_forward(
        blocks, places_near(section_index), table_rows, targets_col, shard_rows
    )
    stats = stats[:, :3].T
    block_max = stats[0]
    stats = spread_small(stats)
    soft_pull, hard_pull = head_pull(exps, targets_col, table_rows)
    highest = jnp.max(stats[:, 0], 0)
    merged_sum = jnp.sum(stats[:, 1] * jnp.exp(stats[:, 0] - highest), 0)
    partition = highest + jnp.log(merged_sum)
    target_all = jnp.sum(stats[:, 2], 0)
    loss_part = jnp.sum(counted * (partition - target_all + Z_WEIGHT * partition * partition))
    token_weight = counted / token_total
    pull = token_weight * (1.0 + 2.0 * Z_WEIGHT * partition) * jnp.exp(block_max - partition)
    token_scales = jnp.stack([pull, token_weight], 1)
    grad_rows = pull[:, None] * soft_pull - token_weight[:, None] * hard_pull.astype(jnp.float32)
    grad_parts = lax.all_to_all(
        grad_rows.astype(jnp.bfloat16).reshape(fsdp_count, -1, model_width), FSDP, 0, 0, tiled=True
    )
    table_grad = head_table(exps, token_scales, targets_col, rows_all)
    grad_normed = jnp.sum(grad_parts, 0, dtype=jnp.float32)
    grad_now, d_fgain, d_fbias = jax.vjp(layer_norm, final_rows, head_norm[0:1], head_norm[1:2])[1](
        grad_normed
    )
    layer_parts, vecs_parts = [], []
    for layer in reversed(range(section_count)):
        grad_now, grads, d_vectors, exponent = layer_backward(
            kept[layer], grad_now, layer_sets[layer]
        )
        layer_parts.insert(0, parted_weights(grads, exponent))
        if layer:
            grad_now = after(grad_now, layer_parts[0][-1])
        vecs_parts = d_vectors + vecs_parts
    emb_all = lax.all_gather(grad_now.astype(jnp.bfloat16), FSDP, axis=0, tiled=True)
    table_grad = rows_scattered(table_grad, local_ids.reshape(-1), emb_all)
    small_grad = lax.optimization_barrier(padded_rows(vecs_parts + [d_fgain, d_fbias, grad_now]))
    small_grad = jnp.moveaxis(small_grad.reshape(small_rows, fsdp_count, -1), 1, 0)
    small_grad = jnp.sum(lax.all_to_all(small_grad, FSDP, 0, 0, tiled=True), 0)
    table_grad = (table_grad + swapped(table_grad, "section"))[:shard_rows]
    table_squares = jnp.sum(table_grad * table_grad)
    flushed = summed_weights(layer_parts, table_squares)
    loss_row = jnp.broadcast_to(loss_part, (1, small_grad.shape[1]))
    small_grad = jnp.concatenate([small_grad, loss_row], 0)
    small_grad = small_grad + swapped(small_grad, "section")
    loss_sum = small_grad[-1, 0]
    vecs_grad = lax.dynamic_slice_in_dim(small_grad, section_index * layer_rows, layer_rows, 0)
    norm_grad = small_grad[norm_at:places_at]
    pos_grad = small_grad[places_at : places_at + place_rows]
    weight_grad = flushed
    own_squares = jnp.sum(weight_grad * weight_grad) + jnp.sum(vecs_grad * vecs_grad)
    shared_squares = table_squares + jnp.sum(pos_grad * pos_grad) + jnp.sum(norm_grad * norm_grad)
    device_squares = own_squares + jnp.where(section_index == 0, shared_squares, 0.0)
    square_sum = lax.psum(
        jnp.sum(spread_small(jnp.full((8, 128), device_squares)), 0)[0, 0], "section"
    )
    clip_norm = jnp.sqrt(square_sum)
    factor = jnp.minimum(1.0, CLIP_NORM / (clip_norm + 1e-06))

    new_moms = [
        MOMENTUM * moments_t[n] + factor * weight_grad[starts[n] : starts[n + 1]] for n in range(4)
    ]
    widest = max(widths)
    padded = jnp.stack([jnp.pad(mom, ((0, widest - mom.shape[0]), (0, 0))) for mom in new_moms])
    padded = (padded * MOMENT_SCALE).astype(jnp.float16)
    padded = padded.reshape(4, 2, widest // 2, model_width)
    sent = lax.all_to_all(padded, "section", 1, 1, tiled=True)
    sent = sent.reshape(4 * section_count, widest // 2, model_width)
    held = lax.all_to_all(sent, SPOTS, 0, 0, tiled=True).reshape(-1, model_width)
    held = held.astype(jnp.float32) * (1.0 / MOMENT_SCALE)
    high, lower = halves_of(held)
    crossed = contract_rows(high, lower)
    gram = contract_rows(high, high) + (crossed + crossed.T) + contract_rows(lower, lower)
    product = newton_product(gram_summed(gram))
    turned = jnp.matmul(held, product, precision=lax.Precision.HIGH).astype(jnp.float16)
    turned = turned.reshape(4 * section_count, widest // 2, model_width)
    back = lax.all_to_all(turned, SPOTS, 0, 0, tiled=True)
    back = back.reshape(4, section_count, widest // 2, model_width)
    back = lax.all_to_all(back, "section", 1, 1, tiled=True).reshape(4, widest, model_width)
    back = back.astype(jnp.float32)

    embed_new, embed_m_new, embed_v_new = adam_step(
        embed_table, factor * table_grad, embed_m, embed_v, RATE_EMBED
    )
    pos_new, pos_m_new, pos_v_new = adam_step(pos_table, factor * pos_grad, pos_m, pos_v, RATE_POS)
    norm_new, norm_m_new, norm_v_new = adam_step(
        final_norm, factor * norm_grad, norm_m, norm_v, RATE_VEC
    )
    vecs_new, vecs_m_new, vecs_v_new = adam_step(
        layer_vecs, factor * vecs_grad[None], vecs_m, vecs_v, RATE_VEC
    )
    results = []
    for number in range(4):
        column_factor = math.sqrt(widths[number] * fsdp_count / model_width)
        new_master = masters_t[number] - MUON_RATE * (
            column_factor * back[number, : widths[number]] + MUON_DECAY * masters_t[number]
        )
        new_master = new_master.T[None]
        results.append((new_master, new_master.astype(jnp.bfloat16), new_moms[number].T[None]))
    return (
        loss_sum,
        clip_norm,
        embed_new,
        embed_new.astype(jnp.bfloat16),
        embed_m_new,
        embed_v_new,
        pos_new,
        pos_m_new,
        pos_v_new,
        *results[0],
        *results[1],
        *results[2],
        *results[3],
        vecs_new,
        vecs_m_new,
        vecs_v_new,
        norm_new,
        norm_m_new,
        norm_v_new,
    )


def inner_mesh(mesh):
    section_count, fsdp_count = mesh.devices.shape
    parts = {16: (4, 2, 1, 2), 64: (4, 2, 2, 4)}.get(fsdp_count, (4, 2, fsdp_count // 8, 1))
    return Mesh(mesh.devices.reshape((section_count,) + parts), ("section",) + FSDP)


def solution(mesh):
    ids = P("section", FSDP, None)
    rows = P(FSDP, None)
    cols = P(None, FSDP)
    layer = P("section", None, FSDP)
    in_specs = (ids, ids, P()) + (rows,) * 3 + (cols,) * 3 + (layer,) * 11 + (cols,) * 3
    out_specs = (P(), P()) + (rows,) * 4 + (cols,) * 3 + (layer,) * 15 + (cols,) * 3
    return jax.shard_map(
        shards, mesh=inner_mesh(mesh), in_specs=in_specs, out_specs=out_specs, check_vma=False
    )
```

```python
import functools
import math

import jax
import jax.numpy as jnp
from jax import lax
from jax.experimental import pallas as pl
from jax.experimental.pallas import tpu as pltpu
from jax.sharding import Mesh
from jax.sharding import PartitionSpec as P

HD = 64
STEP = 10


LN_EPS = 1e-05
NEG_FILL = -1e30
Z_WEIGHT = 0.01
CLIP_NORM = 0.02
MOMENTUM = 0.5
MUON_RATE = 0.7
MUON_DECAY = 0.01
ADAM_ONE = 0.9
ADAM_TWO = 0.95
ADAM_EPS = 1e-08
ADAM_DECAY = 0.1
RATE_EMBED = 0.12
RATE_POS = 0.1
RATE_VEC = 0.2
NEWTON_COEFS = (3.4445, -4.775, 2.0315)
FSDP = ("za", "yb", "yc", "xd")
SPOTS = ("za", "yb")
GROUP = ("section", "yc", "xd")
NOTE = 8
UPPER = ((0, 0), (0, 1), (0, 2), (1, 1), (1, 2), (2, 2))
VMEM_BYTES = 56 * 1024 * 1024


def swapped(block, axis):
    size = lax.axis_size(axis)
    return lax.ppermute(block, axis, [(i, size - 1 - i) for i in range(size)])


def spread_small(block):
    count = lax.axis_size(FSDP)
    copies = jnp.broadcast_to(block[None], (count,) + block.shape)
    return lax.all_to_all(copies, FSDP, 0, 0, tiled=True)


def span():
    return (lax.axis_size("za"), lax.axis_size(("yb", "yc")), lax.axis_size("xd"))


def route(level, distance):
    za, yb, xd = span()
    pairs = []
    for section in range(2):
        for place in range(za * yb * xd):
            a, b, c = place // (yb * xd), place // xd % yb, place % xd
            if level == 2:
                a = (a + distance) % za
            elif section == level:
                b = (b + distance) % yb
            else:
                c = (c + distance) % xd
            start = section * za * yb * xd
            pairs.append((start + place, start + (a * yb + b) * xd + c))
    return pairs


def moved(block, level, distance=1):
    return lax.ppermute(block, ("section",) + FSDP, route(level, distance))


def pick(block, axis, index):
    return lax.dynamic_index_in_dim(block, index, axis, keepdims=False)


def nothing_of(*arrays):
    return sum(jnp.sum(array[(slice(0, 1),) * array.ndim].astype(jnp.float32)) * 0.0 for array in arrays)


def after(value, *others):
    return value + nothing_of(*others).astype(value.dtype)


def column_near(block):
    return jnp.stack([block] + [moved(block, 2, -k) for k in range(1, span()[0])])


def plane_near(column):
    return jnp.stack([column] + [moved(column, 1, -k) for k in range(1, span()[2])])


def planes_near(plane):
    return [plane] + [moved(plane, 0, -k) for k in range(1, span()[1])]


def gathered_near(block):
    return planes_near(plane_near(column_near(block)))


def places_near(section):
    za, yb, xd = span()
    a, b, c = lax.axis_index("za"), lax.axis_index(("yb", "yc")), lax.axis_index("xd")
    owners = jnp.arange(za * yb * xd, dtype=jnp.int32)
    high = (owners // (yb * xd) - a) % za
    row, col = (owners // xd % yb - b) % yb, (owners % xd - c) % xd
    far, near = jnp.where(section == 0, row, col), jnp.where(section == 0, col, row)
    return (far * xd + near) * za + high


def assemble_kernel(widths, count, spot_ref, *refs):
    sources, outs = refs[: -len(widths)], refs[-len(widths) :]
    owner = pl.program_id(0)
    each, half = sources[0].shape[0], sources[0].shape[2]
    for number, source in enumerate(sources):
        kind = number // (len(sources) // 2)
        piece = number % (len(sources) // 2)
        place = spot_ref[kind * count + owner]
        for side in range(2):

            @pl.when((place // each == piece) & (spot_ref[2 * count + kind] == side))
            def _(source=source, place=place, side=side):
                start = 0
                for out, width in zip(outs, widths):
                    out[:, side * half : (side + 1) * half] = source[
                        place % each, start : start + width, :
                    ]
                    start += width


def assembled(own, other, widths):
    section = lax.axis_index("section")
    count = lax.axis_size(FSDP)
    rows, half = own[0].shape[-2:]
    pieces = [piece.reshape(-1, rows, half) for piece in own + other]
    if any(width % 16 for width in widths):
        sides = []
        for side, parts in ((section, pieces[: len(own)]), (1 - section, pieces[len(own) :])):
            sides.append(jnp.take(jnp.concatenate(parts), places_near(side), axis=0))
        first_side = section == 0
        left = jnp.where(first_side, sides[0], sides[1])
        right = jnp.where(first_side, sides[1], sides[0])
        whole = jnp.concatenate([left, right], -1)
        starts = [sum(widths[:n]) for n in range(5)]
        return [whole[:, starts[n] : starts[n + 1]].reshape(-1, 2 * half) for n in range(4)]
    sides = jnp.stack([section, 1 - section])
    spots = jnp.concatenate([places_near(section), places_near(1 - section), sides])
    return pl.pallas_call(
        functools.partial(assemble_kernel, tuple(widths), count),
        grid_spec=pltpu.PrefetchScalarGridSpec(
            num_scalar_prefetch=1,
            grid=(count,),
            in_specs=[pl.BlockSpec(piece.shape, lambda step, spot: (0, 0, 0)) for piece in pieces],
            out_specs=[
                pl.BlockSpec((width, 2 * half), lambda step, spot: (step, 0)) for width in widths
            ],
        ),
        out_shape=[
            jax.ShapeDtypeStruct((count * width, 2 * half), jnp.bfloat16) for width in widths
        ],
        compiler_params=pltpu.CompilerParams(vmem_limit_bytes=VMEM_BYTES),
        cost_estimate=pl.CostEstimate(
            flops=0, bytes_accessed=8 * count * rows * half, transcendentals=0
        ),
    )(spots.astype(jnp.int32), *pieces)


def exponent_for(bound):
    return jnp.floor(14.5 - jnp.log2(jnp.maximum(bound, 1e-30)))


def coded(values, exponent):
    rows = lax.broadcasted_iota(jnp.int32, values.shape, values.ndim - 2)
    noted = rows >= values.shape[-2] - NOTE
    return jnp.where(noted, exponent, values * jnp.exp2(exponent)).astype(jnp.float16)


def exponent_in(block):
    return block[(0,) * (block.ndim - 2) + (block.shape[-2] - 1, 0)].astype(jnp.float32)


def added(kept, came):
    first, second = exponent_in(kept), exponent_in(came)
    total = kept.astype(jnp.float32) * jnp.exp2(-first) + came.astype(jnp.float32) * jnp.exp2(
        -second
    )
    return coded(total, jnp.minimum(first, second) - 1.0)


def planes_cut(block):
    first_side = lax.axis_index("section") == 0
    sizes = span()
    block = block.reshape(sizes + block.shape[1:])
    b, c = lax.axis_index(("yb", "yc")), lax.axis_index("xd")
    parts = []
    for distance in range(sizes[1]):
        row, col = (b + distance) % sizes[1], (c + distance) % sizes[2]
        parts.append(jnp.where(first_side, pick(block, 1, row), pick(block, 2, col)))
    return parts


def planes_reduced(parts, add):
    total = parts[0]
    for distance in range(1, len(parts)):
        total = add(total, moved(parts[distance], 0, distance))
    return total


def plane_reduced(plane, add):
    first_side = lax.axis_index("section") == 0
    inner = jnp.where(first_side, lax.axis_index("xd"), lax.axis_index(("yb", "yc")))
    total = pick(plane, 1, inner)
    for distance in range(1, span()[2]):
        sent = pick(plane, 1, (inner + distance) % span()[2])
        total = add(total, moved(sent, 1, distance))
    return total


def column_parts(column):
    a = lax.axis_index("za")
    parts = [pick(column, 0, a)]
    for distance in range(1, span()[0]):
        parts.append(moved(pick(column, 0, (a + distance) % span()[0]), 2, distance))
    return parts


def decoded(block):
    return block[..., :-NOTE, :].astype(jnp.float32) * jnp.exp2(-exponent_in(block))


def column_sums(column):
    return sum(part.astype(jnp.float32) for part in column_parts(column))


def parted_weights(grads, exponent):
    own = [grad.reshape(lax.axis_size(FSDP), -1, grad.shape[-1]) for grad in grads]
    note = jnp.broadcast_to(exponent.astype(jnp.float16), (own[0].shape[0], NOTE, own[0].shape[2]))
    return planes_cut(jnp.concatenate(own + [note], 1))


def summed_weights(parts_early, parts_late, *before):
    first_side = lax.axis_index("section") == 0
    halves = [sum(decoded(part) for part in parts) for parts in (parts_early, parts_late)]
    halves[0] = after(halves[0], *before)
    kept = jnp.where(first_side, halves[0], halves[1])
    came = swapped(jnp.where(first_side, halves[1], halves[0]), "section")
    return jnp.where(
        first_side, jnp.concatenate([kept, came], 1), jnp.concatenate([came, kept], 1)
    )


def gram_summed(gram):
    tile = gram.shape[0] // 3
    blocks = [gram[i * tile : (i + 1) * tile, j * tile : (j + 1) * tile] for i, j in UPPER]
    near, far = jnp.stack(blocks[:3]), jnp.stack(blocks[3:])
    if lax.axis_size(GROUP) != 4:
        return lax.psum(jnp.concatenate([near, far]), GROUP)
    first_side = lax.axis_index("section") == 0
    kept, gone = jnp.where(first_side, near, far), jnp.where(first_side, far, near)
    kept = kept + swapped(gone, "section")
    kept = kept + swapped(kept, "xd")
    came = swapped(kept, "section")
    return jnp.where(first_side, jnp.concatenate([kept, came]), jnp.concatenate([came, kept]))


def layer_norm(values, gain_row, bias_row):
    average = jnp.mean(values, -1, keepdims=True)
    centered = values - average
    variance = jnp.mean(centered * centered, -1, keepdims=True)
    return centered * lax.rsqrt(variance + LN_EPS) * gain_row + bias_row


def split_vectors(vectors):
    rows = [vectors[number : number + 1] for number in range(12)]
    return (*rows[:7], jnp.concatenate(rows[7:11], 1), rows[11])


def contract_rows(left_mat, right_mat):
    return lax.dot_general(
        left_mat, right_mat, (((0,), (0,)), ((), ())), preferred_element_type=jnp.float32
    )


def contract_cols(left_mat, right_mat):
    return lax.dot_general(
        left_mat, right_mat, (((1,), (1,)), ((), ())), preferred_element_type=jnp.float32
    )


def plain_dot(left_mat, right_mat):
    return jnp.dot(left_mat, right_mat, preferred_element_type=jnp.float32)


def with_other(*values):
    joined = jnp.concatenate(values, 1)
    return jnp.concatenate([joined, swapped(joined, "section")], 0)


def own_half(values):
    half = values.shape[1] // 2
    return lax.dynamic_slice_in_dim(values, lax.axis_index("section") * half, half, 1)


def other_half(values):
    half = values.shape[1] // 2
    return lax.dynamic_slice_in_dim(values, (1 - lax.axis_index("section")) * half, half, 1)


def largest(values):
    return jnp.max(jnp.abs(values)).astype(jnp.float32)


def gelu_tanh(values):
    return jax.nn.gelu(values, approximate=True)


def layer_forward(inputs, weights):
    qkv_t, proj_t, fc_t, down_t, vectors = weights
    g_one, b_one, q_bias, v_bias, p_bias, g_two, b_two, f_bias, d_bias = split_vectors(vectors)
    seq_len, model_width = inputs.shape
    head_count = model_width // HD
    factor = HD ** (-0.5)
    normed_a = layer_norm(inputs, g_one, b_one).astype(jnp.bfloat16)
    bias_qkv = jnp.concatenate([q_bias, jnp.zeros_like(q_bias), v_bias], 1)
    qkv_rows = (contract_cols(normed_a, qkv_t) + bias_qkv).astype(jnp.bfloat16)
    queries = qkv_rows[:, :model_width].reshape(seq_len, head_count, HD)
    keys_all = qkv_rows[:, model_width : 2 * model_width].reshape(seq_len, head_count, HD)
    values_all = qkv_rows[:, 2 * model_width :].reshape(seq_len, head_count, HD)
    scores = (
        jnp.einsum("qhd,khd->hqk", queries, keys_all, preferred_element_type=jnp.float32) * factor
    )
    causal = lax.broadcasted_iota(jnp.int32, (seq_len, seq_len), 0) >= lax.broadcasted_iota(
        jnp.int32, (seq_len, seq_len), 1
    )
    attn_probs = jax.nn.softmax(jnp.where(causal, scores, NEG_FILL), axis=-1)
    probs_low = attn_probs.astype(jnp.bfloat16)
    attended = jnp.einsum("hqk,khd->qhd", probs_low, values_all, preferred_element_type=jnp.float32)
    attended = attended.reshape(seq_len, model_width).astype(jnp.bfloat16)
    after_attn = inputs + contract_cols(attended, proj_t) + p_bias
    normed_b = layer_norm(after_attn, g_two, b_two).astype(jnp.bfloat16)
    hidden_pre = contract_cols(normed_b, fc_t) + f_bias
    hidden_low = gelu_tanh(hidden_pre).astype(jnp.bfloat16)
    outputs = after_attn + plain_dot(hidden_low, down_t) + d_bias
    saved = (
        inputs,
        normed_a,
        queries,
        keys_all,
        values_all,
        attn_probs,
        probs_low,
        attended,
        after_attn,
        normed_b,
        hidden_pre,
        with_other(hidden_low, normed_a, attended, normed_b),
    )
    return (outputs, saved)


def layer_backward(saved, grad_out, weights, nothing):
    qkv_t, proj_t, fc_t, down_t, vectors = weights
    g_one, b_one, q_bias, v_bias, p_bias, g_two, b_two, f_bias, d_bias = split_vectors(vectors)
    (
        inputs,
        normed_a,
        queries,
        keys_all,
        values_all,
        attn_probs,
        probs_low,
        attended,
        after_attn,
        normed_b,
        hidden_pre,
        early,
    ) = saved
    seq_len, model_width = inputs.shape
    factor = HD ** (-0.5)
    grad_mlp = grad_out.astype(jnp.bfloat16)
    d_dbias = jnp.sum(grad_mlp, 0, keepdims=True, dtype=jnp.float32)
    grad_hidden = contract_cols(grad_mlp, down_t)
    grad_pre = jax.vjp(gelu_tanh, hidden_pre)[1](grad_hidden)[0].astype(jnp.bfloat16)
    d_fbias = jnp.sum(grad_pre, 0, keepdims=True, dtype=jnp.float32)
    grad_nb = plain_dot(grad_pre, fc_t)
    ln_two = jax.vjp(layer_norm, after_attn, g_two, b_two)[1](grad_nb)
    grad_mid = grad_out + ln_two[0]
    grad_attn = grad_mid.astype(jnp.bfloat16)
    d_pbias = jnp.sum(grad_attn, 0, keepdims=True, dtype=jnp.float32)
    grad_att = plain_dot(grad_attn, proj_t).reshape(queries.shape).astype(jnp.bfloat16)
    grad_probs = jnp.einsum(
        "qhd,khd->hqk", grad_att, values_all, preferred_element_type=jnp.float32
    )
    grad_vals = jnp.einsum("hqk,qhd->khd", probs_low, grad_att, preferred_element_type=jnp.float32)
    grad_scores = attn_probs * (grad_probs - jnp.sum(grad_probs * attn_probs, -1, keepdims=True))
    grad_scores = grad_scores.astype(jnp.bfloat16)
    grad_q = (
        jnp.einsum("hqk,khd->qhd", grad_scores, keys_all, preferred_element_type=jnp.float32)
        * factor
    )
    grad_k = (
        jnp.einsum("hqk,qhd->khd", grad_scores, queries, preferred_element_type=jnp.float32)
        * factor
    )
    grad_qkv = jnp.concatenate(
        [
            grad_q.reshape(seq_len, model_width),
            grad_k.reshape(seq_len, model_width),
            grad_vals.reshape(seq_len, model_width),
        ],
        -1,
    ).astype(jnp.bfloat16)
    qkv_sums = jnp.sum(grad_qkv, 0, keepdims=True, dtype=jnp.float32)
    late = with_other(grad_qkv + nothing, grad_attn, grad_pre, grad_mlp)
    wide = hidden_pre.shape[1]

    def taken(block, start, width):
        return block[:, start : start + width]

    products = (
        (taken(late, 0, 3 * model_width), taken(early, wide, model_width)),
        (taken(late, 3 * model_width, model_width), taken(early, wide + model_width, model_width)),
        (taken(late, 4 * model_width, wide), taken(early, wide + 2 * model_width, model_width)),
        (taken(early, 0, wide), taken(late, 4 * model_width + wide, model_width)),
    )
    bound = late.shape[0] * largest(early) * largest(late)
    exponent = exponent_for(bound)
    scale = jnp.exp2(exponent)
    d_qkv, d_proj, d_fc, d_down = (
        (contract_rows(left, own_half(right)) * scale).astype(jnp.float16)
        for left, right in products
    )
    grad_na = plain_dot(grad_qkv, qkv_t)
    ln_one = jax.vjp(layer_norm, inputs, g_one, b_one)[1](grad_na)
    grad_in = grad_mid + ln_one[0]
    d_vectors = [
        ln_one[1],
        ln_one[2],
        qkv_sums[:, :model_width],
        qkv_sums[:, 2 * model_width :],
        d_pbias,
        ln_two[1],
        ln_two[2],
        *(d_fbias[:, n * model_width : (n + 1) * model_width] for n in range(4)),
        d_dbias,
    ]
    return (grad_in, (d_qkv, d_proj, d_fc, d_down), d_vectors, exponent)


def adam_step(weights_in, gradient, first_mom, second_mom, step_rate):
    first_new = ADAM_ONE * first_mom + (1.0 - ADAM_ONE) * gradient
    second_new = ADAM_TWO * second_mom + (1.0 - ADAM_TWO) * gradient * gradient
    first_hat = first_new / (1.0 - ADAM_ONE**STEP)
    second_hat = second_new / (1.0 - ADAM_TWO**STEP)
    weights_new = weights_in - step_rate * (
        first_hat / (jnp.sqrt(second_hat) + ADAM_EPS) + ADAM_DECAY * weights_in
    )
    return (weights_new, first_new, second_new)


def halves_of(values):
    high = lax.reduce_precision(values, 8, 7)
    return (high.astype(jnp.bfloat16), (values - high).astype(jnp.bfloat16))


def newton_kernel(gram_ref, out_ref, pair_a, pair_b, gram_now, poly, product):
    tile = gram_ref.shape[1]
    count = 3
    width = count * tile
    a, b, c = NEWTON_COEFS
    rows = lax.broadcasted_iota(jnp.int32, (width, width), 0)
    cols = lax.broadcasted_iota(jnp.int32, (width, width), 1)
    diagonal = rows == cols

    def store_pair(pair, values):
        for part in range(3):
            pair[part] = values.astype(jnp.bfloat16)
            values = values - pair[part].astype(jnp.float32)

    def multiply(left, right, write, terms=2):
        for i in range(count):
            row_at = slice(i * tile, (i + 1) * tile)
            for j in range(i, count):
                col_at = slice(j * tile, (j + 1) * tile)
                block = jnp.zeros((tile, tile), jnp.float32)
                for part in reversed(range(terms)):
                    for other in reversed(range(terms - part)):
                        block += plain_dot(left[part, row_at, :], right[other, :, col_at])
                write(row_at, col_at, block)
                if i != j:
                    write(col_at, row_at, block.T)

    def into(ref):
        def write(row_at, col_at, block):
            ref[row_at, col_at] = block

        return write

    for number, (i, j) in enumerate(UPPER):
        row_at, col_at = slice(i * tile, (i + 1) * tile), slice(j * tile, (j + 1) * tile)
        gram_now[row_at, col_at] = gram_ref[number]
        if i != j:
            gram_now[col_at, row_at] = gram_ref[number].T
    full = gram_now[...]
    trace = jnp.sum(jnp.where(diagonal, full, 0.0))
    inverse = 1.0 / (jnp.sqrt(jnp.full((1, 1), trace, jnp.float32)) + 1e-07)
    gram_now[...] = full * (inverse * inverse)

    def step_poly():
        store_pair(pair_a, gram_now[...])
        multiply(pair_a, pair_a, into(poly))
        poly[...] = jnp.where(diagonal, a, 0.0) + b * gram_now[...] + c * poly[...]
        store_pair(pair_b, poly[...])

    def step_gram(terms):
        multiply(pair_a, pair_b, into(gram_now), terms)
        store_pair(pair_a, gram_now[...])
        multiply(pair_a, pair_b, into(gram_now), terms)

    def step_product():
        store_pair(pair_a, product[...])
        multiply(pair_a, pair_b, into(product))

    step_poly()
    step_gram(3)
    product[...] = poly[...]

    @pl.loop(0, 3)
    def _(iteration):
        step_poly()
        step_gram(2)
        step_product()

    step_poly()
    step_product()
    out_ref[...] = product[...] * inverse


def newton_product(gram_blocks):
    width = 3 * gram_blocks.shape[1]
    square = (width, width)
    return pl.pallas_call(
        newton_kernel,
        out_shape=jax.ShapeDtypeStruct(square, jnp.float32),
        in_specs=[pl.BlockSpec(memory_space=pltpu.VMEM)],
        out_specs=pl.BlockSpec(memory_space=pltpu.VMEM),
        scratch_shapes=[
            pltpu.VMEM((3,) + square, jnp.bfloat16),
            pltpu.VMEM((3,) + square, jnp.bfloat16),
            pltpu.VMEM(square, jnp.float32),
            pltpu.VMEM(square, jnp.float32),
            pltpu.VMEM(square, jnp.float32),
        ],
        compiler_params=pltpu.CompilerParams(vmem_limit_bytes=48 * 1024 * 1024),
        cost_estimate=pl.CostEstimate(
            flops=17 * 4 * width**3, bytes_accessed=8 * width * width, transcendentals=0
        ),
    )(gram_blocks)


def head_forward_kernel(
    shard_rows, spot_ref, one_ref, two_ref, table_ref, target_ref, exp_ref, stat_ref, row_ref
):
    rows = jnp.concatenate([one_ref[0], two_ref[0]], 0)
    row_ref[...] = rows
    logits = contract_cols(rows, table_ref[...])
    cols = lax.broadcasted_iota(jnp.int32, logits.shape, 1)
    logits = jnp.where(cols < shard_rows, logits, NEG_FILL)
    highest = jnp.max(logits, -1, keepdims=True)
    exps = jnp.exp(logits - highest)
    total = jnp.sum(exps, -1, keepdims=True)
    target = jnp.sum(jnp.where(cols == target_ref[...], logits, 0.0), -1, keepdims=True)
    exp_ref[...] = exps.astype(jnp.bfloat16)
    lanes = lax.broadcasted_iota(jnp.int32, stat_ref.shape, 1)
    stat_ref[...] = jnp.where(lanes == 0, highest, jnp.where(lanes == 1, total, target))


def head_forward(blocks, places, table, targets, shard_rows):
    number, tokens, width = blocks.shape
    count = number * tokens
    vocab = table.shape[0]
    step = 2 * tokens
    return pl.pallas_call(
        functools.partial(head_forward_kernel, shard_rows),
        grid_spec=pltpu.PrefetchScalarGridSpec(
            num_scalar_prefetch=1,
            grid=(number // 2,),
            in_specs=[
                pl.BlockSpec((1, tokens, width), lambda i, spot: (spot[2 * i], 0, 0)),
                pl.BlockSpec((1, tokens, width), lambda i, spot: (spot[2 * i + 1], 0, 0)),
                pl.BlockSpec((vocab, width), lambda i, spot: (0, 0)),
                pl.BlockSpec((step, 1), lambda i, spot: (i, 0)),
            ],
            out_specs=[
                pl.BlockSpec((step, vocab), lambda i, spot: (i, 0)),
                pl.BlockSpec((step, 128), lambda i, spot: (i, 0)),
                pl.BlockSpec((step, width), lambda i, spot: (i, 0)),
            ],
        ),
        out_shape=[
            jax.ShapeDtypeStruct((count, vocab), jnp.bfloat16),
            jax.ShapeDtypeStruct((count, 128), jnp.float32),
            jax.ShapeDtypeStruct((count, width), jnp.bfloat16),
        ],
        compiler_params=pltpu.CompilerParams(vmem_limit_bytes=VMEM_BYTES),
        cost_estimate=pl.CostEstimate(
            flops=2 * count * vocab * width,
            bytes_accessed=2 * (vocab * width + count * (width + vocab)),
            transcendentals=count * vocab,
        ),
    )(places, blocks, blocks, table, targets)


def head_pull_kernel(exp_ref, target_ref, table_ref, soft_ref, hard_ref):
    exps = exp_ref[...]
    cols = lax.broadcasted_iota(jnp.int32, exps.shape, 1)
    chosen = jnp.where(cols == target_ref[...], 1.0, 0.0).astype(jnp.bfloat16)
    soft_ref[...] = plain_dot(exps, table_ref[...]).astype(jnp.bfloat16)
    hard_ref[...] = plain_dot(chosen, table_ref[...]).astype(jnp.bfloat16)


def head_pull(exps, targets, table):
    count, vocab = exps.shape
    width = table.shape[1]
    step = min(256, count)
    return pl.pallas_call(
        head_pull_kernel,
        grid=(count // step,),
        out_shape=[
            jax.ShapeDtypeStruct((count, width), jnp.bfloat16),
            jax.ShapeDtypeStruct((count, width), jnp.bfloat16),
        ],
        in_specs=[
            pl.BlockSpec((step, vocab), lambda i: (i, 0)),
            pl.BlockSpec((step, 1), lambda i: (i, 0)),
            pl.BlockSpec((vocab, width), lambda i: (0, 0)),
        ],
        out_specs=[
            pl.BlockSpec((step, width), lambda i: (i, 0)),
            pl.BlockSpec((step, width), lambda i: (i, 0)),
        ],
        compiler_params=pltpu.CompilerParams(vmem_limit_bytes=VMEM_BYTES),
        cost_estimate=pl.CostEstimate(
            flops=4 * count * vocab * width,
            bytes_accessed=2 * (vocab * width + count * (3 * width + vocab)),
            transcendentals=0,
        ),
    )(exps, targets, table)


def head_table_kernel(exp_ref, token_ref, target_ref, row_ref, grad_ref):
    exps = exp_ref[...].astype(jnp.float32)
    cols = lax.broadcasted_iota(jnp.int32, exps.shape, 1)
    at_target = jnp.where(cols == target_ref[...], token_ref[:, 1:2], 0.0)
    grad_logit = (exps * token_ref[:, 0:1] - at_target).astype(jnp.bfloat16)

    @pl.when(pl.program_id(0) == 0)
    def _():
        grad_ref[...] = jnp.zeros_like(grad_ref)

    grad_ref[...] += contract_rows(grad_logit, row_ref[...])


def head_table(exps, token_scales, targets, rows):
    count, vocab = exps.shape
    width = rows.shape[1]
    step = min(256, count)
    return pl.pallas_call(
        head_table_kernel,
        grid=(count // step,),
        out_shape=jax.ShapeDtypeStruct((vocab, width), jnp.float32),
        in_specs=[
            pl.BlockSpec((step, vocab), lambda i: (i, 0)),
            pl.BlockSpec((step, 2), lambda i: (i, 0)),
            pl.BlockSpec((step, 1), lambda i: (i, 0)),
            pl.BlockSpec((step, width), lambda i: (i, 0)),
        ],
        out_specs=pl.BlockSpec((vocab, width), lambda i: (0, 0)),
        compiler_params=pltpu.CompilerParams(vmem_limit_bytes=VMEM_BYTES),
        cost_estimate=pl.CostEstimate(
            flops=2 * count * vocab * width,
            bytes_accessed=2 * (2 * vocab * width + count * (width + vocab)),
            transcendentals=0,
        ),
    )(exps, token_scales, targets, rows)


def row_scatter_kernel(id_ref, part_ref, total_ref, out_ref):
    @pl.when(pl.program_id(0) == 0)
    def _():
        out_ref[...] = total_ref[...]

    spots = lax.broadcasted_iota(jnp.int32, (out_ref.shape[0], id_ref.shape[1]), 0)
    chosen = jnp.where(spots == id_ref[...], 1.0, 0.0).astype(jnp.bfloat16)
    out_ref[...] += plain_dot(chosen, part_ref[...])


def rows_scattered(total, ids, parts):
    vocab, width = total.shape
    count = parts.shape[0]
    step = min(256, count)
    return pl.pallas_call(
        row_scatter_kernel,
        grid=(count // step,),
        out_shape=jax.ShapeDtypeStruct(total.shape, total.dtype),
        input_output_aliases={2: 0},
        in_specs=[
            pl.BlockSpec((1, step), lambda i: (0, i)),
            pl.BlockSpec((step, width), lambda i: (i, 0)),
            pl.BlockSpec((vocab, width), lambda i: (0, 0)),
        ],
        out_specs=pl.BlockSpec((vocab, width), lambda i: (0, 0)),
        compiler_params=pltpu.CompilerParams(vmem_limit_bytes=VMEM_BYTES),
        cost_estimate=pl.CostEstimate(
            flops=2 * count * vocab * width,
            bytes_accessed=8 * vocab * width + 2 * count * width,
            transcendentals=0,
        ),
    )(ids.reshape(1, count), parts, total)


def to_spots(matrices, code):
    widest = max(matrix.shape[0] for matrix in matrices)
    padded = jnp.stack([jnp.pad(m, ((0, widest - m.shape[0]), (0, 0))) for m in matrices])
    padded = padded.reshape(4, 2, widest // 2, -1)
    if code:
        padded = jnp.pad(padded, ((0, 0), (0, 0), (0, NOTE), (0, 0)))
        padded = coded(padded, exponent_for(jnp.max(jnp.abs(padded))))
    sent = lax.all_to_all(padded, "section", 1, 1, tiled=True)
    sent = sent.reshape((-1,) + sent.shape[2:])
    return lax.all_to_all(sent, SPOTS, 0, 0, tiled=True), sent


def at_spots(held, code):
    if code:
        exponents = held[:, -1:, :1].astype(jnp.float32)
        held = held[:, :-NOTE].astype(jnp.float32) * jnp.exp2(-exponents)
    return held.reshape(-1, held.shape[2])


def from_spots(held):
    back = lax.all_to_all(held.reshape(8, -1, held.shape[1]), SPOTS, 0, 0, tiled=True)
    back = back.reshape((4, 2) + back.shape[1:])
    back = lax.all_to_all(back, "section", 1, 1, tiled=True)
    return back.reshape(4, -1, back.shape[3])


def shards(
    token_ids,
    target_ids,
    true_counts,
    embed_table,
    embed_m,
    embed_v,
    pos_table,
    pos_m,
    pos_v,
    w_qkv,
    w_proj,
    w_fc,
    w_down,
    mom_qkv,
    mom_proj,
    mom_fc,
    mom_down,
    layer_vecs,
    vecs_m,
    vecs_v,
    final_norm,
    norm_m,
    norm_v,
):
    section_index = lax.axis_index("section")
    section_count = lax.axis_size("section")
    fsdp_count = lax.axis_size(FSDP)
    shard_rows, model_width = embed_table.shape
    vocab_start = lax.axis_index(FSDP) * shard_rows
    vocab_rows = -(-shard_rows // 128) * 128
    table_rows = jnp.pad(embed_table.astype(jnp.bfloat16), ((0, vocab_rows - shard_rows), (0, 0)))
    masters_t = [w[0].T for w in (w_qkv, w_proj, w_fc, w_down)]
    moments_t = [m[0].T for m in (mom_qkv, mom_proj, mom_fc, mom_down)]
    widths = [w.shape[0] for w in masters_t]
    starts = [sum(widths[:number]) for number in range(5)]
    layer_rows, place_rows = layer_vecs.shape[1], pos_table.shape[0]
    norm_at = section_count * layer_rows
    places_at = norm_at + final_norm.shape[0]
    small_rows = -(-(places_at + place_rows) // 16) * 16

    def padded_rows(parts):
        missing = small_rows - sum(part.shape[0] for part in parts)
        return jnp.concatenate(parts + [jnp.zeros((missing, parts[0].shape[1]), parts[0].dtype)], 0)

    vecs_both = lax.all_gather(layer_vecs[0].astype(jnp.bfloat16), "section", axis=0, tiled=True)
    token_row = jnp.concatenate([token_ids[0], target_ids[0]], 1)
    token_row = jnp.concatenate([token_row // 256, token_row % 256], 1)
    lanes = layer_vecs.shape[2]
    token_rows = -(-token_row.shape[1] // lanes)
    token_row = jnp.pad(token_row, ((0, 0), (0, token_rows * lanes - token_row.shape[1])))
    token_row = token_row.reshape(token_rows, lanes).astype(jnp.bfloat16)
    small = padded_rows([vecs_both, final_norm.astype(jnp.bfloat16), pos_table.astype(jnp.bfloat16)])
    small = spread_small(jnp.concatenate([small, token_row], 0))
    ids_parts = small[:, small_rows:].astype(jnp.int32).reshape(fsdp_count, -1)
    seq_len = token_ids.shape[2]
    ids_targets = 256 * ids_parts[:, : 2 * seq_len] + ids_parts[:, 2 * seq_len : 4 * seq_len]
    ids_all, targets_all = ids_targets[:, :seq_len], ids_targets[:, seq_len:]
    seq_count = ids_all.shape[0]
    small = jnp.moveaxis(small[:, :small_rows], 0, 1).reshape(small_rows, model_width)
    small = small.astype(jnp.float32)
    head_norm = small[norm_at:places_at]
    positions = small[places_at : places_at + place_rows]
    pack = jnp.concatenate(masters_t, 0).astype(jnp.bfloat16)
    local_ids = ids_all - vocab_start
    inside = (local_ids >= 0) & (local_ids < shard_rows)
    safe_ids = jnp.clip(local_ids, 0, shard_rows - 1)
    contrib = jnp.where(
        inside[..., None], jnp.take(table_rows, safe_ids, axis=0), jnp.zeros((), jnp.bfloat16)
    )
    first_side = section_index == 0
    kept_half = own_half(pack)
    came_half = swapped(other_half(pack), "section")
    blocks = [jnp.where(section_index == layer, kept_half, came_half) for layer in range(2)]
    column_early = after(column_near(blocks[0]), small)
    column_late = column_near(after(lax.optimization_barrier(blocks[1]), contrib))
    rows_plane = planes_reduced(planes_cut(contrib), lax.add)
    planes = [planes_near(plane_near(column_early))]
    planes.append(planes_near(plane_near(after(column_late, rows_plane))))
    rows_in = column_sums(plane_reduced(rows_plane, lax.add))
    layer_sets = []
    for layer, own in enumerate(planes):
        other = [swapped(piece, "section") for piece in own]
        layer_sets.append(
            list(assembled(own, other, widths))
            + [small[layer * layer_rows : (layer + 1) * layer_rows]]
        )


    current = rows_in + positions
    kept = []
    for weights in layer_sets:
        current, saved = layer_forward(current, weights)
        kept.append(saved)
    final_rows = current
    normed_low = layer_norm(final_rows, head_norm[0:1], head_norm[1:2]).astype(jnp.bfloat16)
    blocks = jnp.concatenate(gathered_near(normed_low), 0).reshape((fsdp_count,) + normed_low.shape)
    counts_row = jnp.take(true_counts, section_index, axis=0)
    counted = lax.broadcasted_iota(jnp.int32, (seq_count, seq_len), 1) < counts_row[:, None]
    counted = counted.astype(jnp.float32).reshape(-1)
    token_total = jnp.sum(true_counts).astype(jnp.float32)
    local_targets = targets_all.reshape(-1) - vocab_start
    targets_here = (local_targets >= 0) & (local_targets < shard_rows)
    targets_col = jnp.where(targets_here, local_targets, -1)[:, None]
    exps, stats, rows_all = head_forward(
        blocks, places_near(section_index), table_rows, targets_col, shard_rows
    )
    stats = stats[:, :3].T
    block_max, target_logit = stats[0], stats[2]
    stats = spread_small(stats)
    soft_pull, hard_pull = head_pull(exps, targets_col, table_rows)
    moments_sent = [after(moment, blocks) for moment in moments_t]
    held_moments = at_spots(to_spots(moments_sent, True)[0], True)
    highest = jnp.max(stats[:, 0], 0)
    merged_sum = jnp.sum(stats[:, 1] * jnp.exp(stats[:, 0] - highest), 0)
    partition = highest + jnp.log(merged_sum)
    target_all = jnp.sum(stats[:, 2], 0)
    loss_part = jnp.sum(counted * (partition - target_all + Z_WEIGHT * partition * partition))
    token_weight = counted / token_total
    pull = token_weight * (1.0 + 2.0 * Z_WEIGHT * partition) * jnp.exp(block_max - partition)
    token_scales = jnp.stack([pull, token_weight], 1)
    z_pull = token_weight * (1.0 + 2.0 * Z_WEIGHT * partition)
    at_target = z_pull * jnp.exp(target_all - partition) - token_weight
    at_target = lax.reduce_precision(at_target, 8, 7)
    in_soft = jnp.where(targets_here, jnp.exp(target_logit - block_max), 0.0)
    hard_scale = at_target - pull * lax.reduce_precision(in_soft, 8, 7)
    hard_scale = after(hard_scale, held_moments)
    grad_rows = pull[:, None] * soft_pull.astype(jnp.float32) + hard_scale[:, None] * (
        hard_pull.astype(jnp.float32)
    )
    grad_parts = lax.all_to_all(
        grad_rows.astype(jnp.bfloat16).reshape(fsdp_count, -1, model_width), FSDP, 0, 0, tiled=True
    )
    table_grad = head_table(exps, token_scales, targets_col, rows_all)
    grad_parts = after(grad_parts, table_grad)
    grad_normed = jnp.sum(grad_parts, 0, dtype=jnp.float32)
    grad_now, d_fgain, d_fbias = jax.vjp(layer_norm, final_rows, head_norm[0:1], head_norm[1:2])[1](
        grad_normed
    )
    planes_part, vecs_parts = [], []
    nothing = jnp.zeros((), jnp.bfloat16)
    for layer in reversed(range(section_count)):
        grad_now, grads, d_vectors, exponent = layer_backward(
            kept[layer], grad_now, layer_sets[layer], nothing
        )
        parted = parted_weights(grads, exponent)
        planes_part.insert(0, planes_reduced(parted, added))
        if layer:
            grad_now = after(grad_now, parted[-1])
            column_late = plane_reduced(planes_part[0], added)
            parts_late = column_parts(column_late)
            nothing = nothing_of(column_late).astype(jnp.bfloat16)
        vecs_parts = d_vectors + vecs_parts
    emb_all = lax.all_gather(grad_now.astype(jnp.bfloat16), FSDP, axis=0, tiled=True)
    late_ids = local_ids.reshape(-1) + nothing_of(planes_part[0], *parts_late).astype(
        jnp.int32
    )
    table_grad = rows_scattered(table_grad, late_ids, emb_all)
    small_grad = lax.optimization_barrier(padded_rows(vecs_parts + [d_fgain, d_fbias, grad_now]))
    small_grad = jnp.moveaxis(small_grad.reshape(small_rows, fsdp_count, -1), 1, 0)
    small_grad = jnp.sum(lax.all_to_all(small_grad, FSDP, 0, 0, tiled=True), 0)
    table_grad = (table_grad + swapped(table_grad, "section"))[:shard_rows]
    own_rows = shard_rows // section_count
    table_part = lax.dynamic_slice_in_dim(table_grad, section_index * own_rows, own_rows, 0)
    table_squares = jnp.sum(table_part * table_part)
    parts_early = column_parts(plane_reduced(planes_part[0], added))
    flushed = summed_weights(parts_early, parts_late, table_squares, small_grad)
    loss_row = jnp.broadcast_to(loss_part, (1, small_grad.shape[1]))
    small_grad = jnp.concatenate([small_grad, loss_row], 0)
    small_grad = small_grad + swapped(small_grad, "section")
    loss_sum = small_grad[-1, 0]
    vecs_grad = lax.dynamic_slice_in_dim(small_grad, section_index * layer_rows, layer_rows, 0)
    norm_grad = small_grad[norm_at:places_at]
    pos_grad = small_grad[places_at : places_at + place_rows]
    weight_grad = flushed
    held_grads, set_out = to_spots([weight_grad[starts[n] : starts[n + 1]] for n in range(4)], True)
    held_grads = at_spots(held_grads, True)
    own_squares = jnp.sum(weight_grad * weight_grad) + jnp.sum(vecs_grad * vecs_grad)
    shared_squares = jnp.sum(pos_grad * pos_grad) + jnp.sum(norm_grad * norm_grad)
    device_squares = (
        own_squares + table_squares + jnp.where(section_index == 0, shared_squares, 0.0)
    )
    square_sum = lax.psum(
        jnp.sum(spread_small(jnp.full((8, 128), device_squares)), 0)[0, 0], "section"
    )
    clip_norm = jnp.sqrt(square_sum)
    factor = jnp.minimum(1.0, CLIP_NORM / (clip_norm + 1e-06))

    new_moms = [
        MOMENTUM * moments_t[n] + factor * weight_grad[starts[n] : starts[n + 1]] for n in range(4)
    ]
    held = MOMENTUM * held_moments + factor * held_grads
    high, lower = halves_of(held)
    gram = contract_rows(
        jnp.concatenate([lower, lower, high, high]), jnp.concatenate([lower, high, lower, high])
    )
    product = newton_product(gram_summed(gram))
    turned = jnp.matmul(held, product, precision=lax.Precision.HIGH).astype(jnp.float16)
    back = from_spots(turned)
    back = back.astype(jnp.float32)

    embed_new, embed_m_new, embed_v_new = adam_step(
        embed_table, factor * table_grad, embed_m, embed_v, RATE_EMBED
    )
    pos_new, pos_m_new, pos_v_new = adam_step(pos_table, factor * pos_grad, pos_m, pos_v, RATE_POS)
    norm_new, norm_m_new, norm_v_new = adam_step(
        final_norm, factor * norm_grad, norm_m, norm_v, RATE_VEC
    )
    vecs_new, vecs_m_new, vecs_v_new = adam_step(
        layer_vecs, factor * vecs_grad[None], vecs_m, vecs_v, RATE_VEC
    )
    results = []
    for number in range(4):
        column_factor = math.sqrt(widths[number] * fsdp_count / model_width)
        new_master = masters_t[number] - MUON_RATE * (
            column_factor * back[number, : widths[number]] + MUON_DECAY * masters_t[number]
        )
        new_master = new_master.T[None]
        results.append((new_master, new_master.astype(jnp.bfloat16), new_moms[number].T[None]))
    return (
        loss_sum,
        clip_norm,
        embed_new,
        embed_new.astype(jnp.bfloat16),
        embed_m_new,
        embed_v_new,
        pos_new,
        pos_m_new,
        pos_v_new,
        *results[0],
        *results[1],
        *results[2],
        *results[3],
        vecs_new,
        vecs_m_new,
        vecs_v_new,
        norm_new,
        norm_m_new,
        norm_v_new,
    )


def inner_mesh(mesh):
    section_count, fsdp_count = mesh.devices.shape
    parts = {16: (4, 2, 1, 2), 64: (4, 2, 2, 4)}.get(fsdp_count, (4, 2, fsdp_count // 8, 1))
    return Mesh(mesh.devices.reshape((section_count,) + parts), ("section",) + FSDP)


def solution(mesh):
    ids = P("section", FSDP, None)
    rows = P(FSDP, None)
    cols = P(None, FSDP)
    layer = P("section", None, FSDP)
    in_specs = (ids, ids, P()) + (rows,) * 3 + (cols,) * 3 + (layer,) * 11 + (cols,) * 3
    out_specs = (P(), P()) + (rows,) * 4 + (cols,) * 3 + (layer,) * 15 + (cols,) * 3
    return jax.shard_map(
        shards, mesh=inner_mesh(mesh), in_specs=in_specs, out_specs=out_specs, check_vma=False
    )
```

```python
import functools
import math

import jax
import jax.numpy as jnp
from jax import lax
from jax.experimental import pallas as pl
from jax.experimental.pallas import tpu as pltpu
from jax.sharding import Mesh
from jax.sharding import PartitionSpec as P

HD = 64
STEP = 10


LN_EPS = 1e-05
NEG_FILL = -1e30
Z_WEIGHT = 0.01
CLIP_NORM = 0.02
MOMENTUM = 0.5
MUON_RATE = 0.7
MUON_DECAY = 0.01
ADAM_ONE = 0.9
ADAM_TWO = 0.95
ADAM_EPS = 1e-08
ADAM_DECAY = 0.1
RATE_EMBED = 0.12
RATE_POS = 0.1
RATE_VEC = 0.2
NEWTON_COEFS = (3.4445, -4.775, 2.0315)
FSDP = ("za", "yb", "yc", "xd")
SPOTS = ("za", "yb")
GROUP = ("section", "yc", "xd")
NOTE = 8
UPPER = ((0, 0), (0, 1), (0, 2), (1, 1), (1, 2), (2, 2))
VMEM_BYTES = 56 * 1024 * 1024


def swapped(block, axis):
    size = lax.axis_size(axis)
    return lax.ppermute(block, axis, [(i, size - 1 - i) for i in range(size)])


def spread_small(block):
    count = lax.axis_size(FSDP)
    copies = jnp.broadcast_to(block[None], (count,) + block.shape)
    return lax.all_to_all(copies, FSDP, 0, 0, tiled=True)


def span():
    return (lax.axis_size("za"), lax.axis_size(("yb", "yc")), lax.axis_size("xd"))


def route(level, distance):
    za, yb, xd = span()
    pairs = []
    for section in range(2):
        for place in range(za * yb * xd):
            a, b, c = place // (yb * xd), place // xd % yb, place % xd
            if level == 2:
                a = (a + distance) % za
            elif section == level:
                b = (b + distance) % yb
            else:
                c = (c + distance) % xd
            start = section * za * yb * xd
            pairs.append((start + place, start + (a * yb + b) * xd + c))
    return pairs


def moved(block, level, distance=1):
    return lax.ppermute(block, ("section",) + FSDP, route(level, distance))


def pick(block, axis, index):
    return lax.dynamic_index_in_dim(block, index, axis, keepdims=False)


def nothing_of(*arrays):
    return sum(jnp.sum(array[(slice(0, 1),) * array.ndim].astype(jnp.float32)) * 0.0 for array in arrays)


def after(value, *others):
    return value + nothing_of(*others).astype(value.dtype)


def column_near(block):
    return jnp.stack([block] + [moved(block, 2, -k) for k in range(1, span()[0])])


def plane_near(column):
    return jnp.stack([column] + [moved(column, 1, -k) for k in range(1, span()[2])])


def planes_near(plane):
    return [plane] + [moved(plane, 0, -k) for k in range(1, span()[1])]


def gathered_near(block):
    return planes_near(plane_near(column_near(block)))


def places_near(section):
    za, yb, xd = span()
    a, b, c = lax.axis_index("za"), lax.axis_index(("yb", "yc")), lax.axis_index("xd")
    owners = jnp.arange(za * yb * xd, dtype=jnp.int32)
    high = (owners // (yb * xd) - a) % za
    row, col = (owners // xd % yb - b) % yb, (owners % xd - c) % xd
    far, near = jnp.where(section == 0, row, col), jnp.where(section == 0, col, row)
    return (far * xd + near) * za + high


def assemble_kernel(widths, count, spot_ref, *refs):
    sources, outs = refs[: -len(widths)], refs[-len(widths) :]
    owner = pl.program_id(0)
    each, half = sources[0].shape[0], sources[0].shape[2]
    for number, source in enumerate(sources):
        kind = number // (len(sources) // 2)
        piece = number % (len(sources) // 2)
        place = spot_ref[kind * count + owner]
        for side in range(2):

            @pl.when((place // each == piece) & (spot_ref[2 * count + kind] == side))
            def _(source=source, place=place, side=side):
                start = 0
                for out, width in zip(outs, widths):
                    out[:, side * half : (side + 1) * half] = source[
                        place % each, start : start + width, :
                    ]
                    start += width


def assembled(own, other, widths):
    section = lax.axis_index("section")
    count = lax.axis_size(FSDP)
    rows, half = own[0].shape[-2:]
    pieces = [piece.reshape(-1, rows, half) for piece in own + other]
    if any(width % 16 for width in widths):
        sides = []
        for side, parts in ((section, pieces[: len(own)]), (1 - section, pieces[len(own) :])):
            sides.append(jnp.take(jnp.concatenate(parts), places_near(side), axis=0))
        first_side = section == 0
        left = jnp.where(first_side, sides[0], sides[1])
        right = jnp.where(first_side, sides[1], sides[0])
        whole = jnp.concatenate([left, right], -1)
        starts = [sum(widths[:n]) for n in range(5)]
        return [whole[:, starts[n] : starts[n + 1]].reshape(-1, 2 * half) for n in range(4)]
    sides = jnp.stack([section, 1 - section])
    spots = jnp.concatenate([places_near(section), places_near(1 - section), sides])
    return pl.pallas_call(
        functools.partial(assemble_kernel, tuple(widths), count),
        grid_spec=pltpu.PrefetchScalarGridSpec(
            num_scalar_prefetch=1,
            grid=(count,),
            in_specs=[pl.BlockSpec(piece.shape, lambda step, spot: (0, 0, 0)) for piece in pieces],
            out_specs=[
                pl.BlockSpec((width, 2 * half), lambda step, spot: (step, 0)) for width in widths
            ],
        ),
        out_shape=[
            jax.ShapeDtypeStruct((count * width, 2 * half), jnp.bfloat16) for width in widths
        ],
        compiler_params=pltpu.CompilerParams(vmem_limit_bytes=VMEM_BYTES),
        cost_estimate=pl.CostEstimate(
            flops=0, bytes_accessed=8 * count * rows * half, transcendentals=0
        ),
    )(spots.astype(jnp.int32), *pieces)


def exponent_for(bound):
    return jnp.floor(14.5 - jnp.log2(jnp.maximum(bound, 1e-30)))


def coded(values, exponent):
    rows = lax.broadcasted_iota(jnp.int32, values.shape, values.ndim - 2)
    noted = rows >= values.shape[-2] - NOTE
    return jnp.where(noted, exponent, values * jnp.exp2(exponent)).astype(jnp.float16)


def exponent_in(block):
    return block[(0,) * (block.ndim - 2) + (block.shape[-2] - 1, 0)].astype(jnp.float32)


def added(kept, came):
    first, second = exponent_in(kept), exponent_in(came)
    total = kept.astype(jnp.float32) * jnp.exp2(-first) + came.astype(jnp.float32) * jnp.exp2(
        -second
    )
    return coded(total, jnp.minimum(first, second) - 1.0)


def planes_cut(block):
    first_side = lax.axis_index("section") == 0
    sizes = span()
    block = block.reshape(sizes + block.shape[1:])
    b, c = lax.axis_index(("yb", "yc")), lax.axis_index("xd")
    parts = []
    for distance in range(sizes[1]):
        row, col = (b + distance) % sizes[1], (c + distance) % sizes[2]
        parts.append(jnp.where(first_side, pick(block, 1, row), pick(block, 2, col)))
    return parts


def planes_reduced(parts, add):
    total = parts[0]
    for distance in range(1, len(parts)):
        total = add(total, moved(parts[distance], 0, distance))
    return total


def plane_reduced(plane, add):
    first_side = lax.axis_index("section") == 0
    inner = jnp.where(first_side, lax.axis_index("xd"), lax.axis_index(("yb", "yc")))
    total = pick(plane, 1, inner)
    for distance in range(1, span()[2]):
        sent = pick(plane, 1, (inner + distance) % span()[2])
        total = add(total, moved(sent, 1, distance))
    return total


def column_parts(column):
    a = lax.axis_index("za")
    parts = [pick(column, 0, a)]
    for distance in range(1, span()[0]):
        parts.append(moved(pick(column, 0, (a + distance) % span()[0]), 2, distance))
    return parts


def decoded(block):
    return block[..., :-NOTE, :].astype(jnp.float32) * jnp.exp2(-exponent_in(block))


def column_sums(column):
    return sum(part.astype(jnp.float32) for part in column_parts(column))


def parted_weights(grads, exponent):
    own = [grad.reshape(lax.axis_size(FSDP), -1, grad.shape[-1]) for grad in grads]
    note = jnp.broadcast_to(exponent.astype(jnp.float16), (own[0].shape[0], NOTE, own[0].shape[2]))
    return planes_cut(jnp.concatenate(own + [note], 1))


def summed_weights(parts_early, parts_late, *before):
    first_side = lax.axis_index("section") == 0
    halves = [sum(decoded(part) for part in parts) for parts in (parts_early, parts_late)]
    halves[0] = after(halves[0], *before)
    kept = jnp.where(first_side, halves[0], halves[1])
    came = swapped(jnp.where(first_side, halves[1], halves[0]), "section")
    return jnp.where(
        first_side, jnp.concatenate([kept, came], 1), jnp.concatenate([came, kept], 1)
    )


def gram_summed(gram):
    tile = gram.shape[0] // 3
    blocks = [gram[i * tile : (i + 1) * tile, j * tile : (j + 1) * tile] for i, j in UPPER]
    near, far = jnp.stack(blocks[:3]), jnp.stack(blocks[3:])
    if lax.axis_size(GROUP) != 4:
        return lax.psum(jnp.concatenate([near, far]), GROUP)
    first_side = lax.axis_index("section") == 0
    kept, gone = jnp.where(first_side, near, far), jnp.where(first_side, far, near)
    kept = kept + swapped(gone, "section")
    kept = kept + swapped(kept, "xd")
    came = swapped(kept, "section")
    return jnp.where(first_side, jnp.concatenate([kept, came]), jnp.concatenate([came, kept]))


def layer_norm(values, gain_row, bias_row):
    average = jnp.mean(values, -1, keepdims=True)
    centered = values - average
    variance = jnp.mean(centered * centered, -1, keepdims=True)
    return centered * lax.rsqrt(variance + LN_EPS) * gain_row + bias_row


def split_vectors(vectors):
    rows = [vectors[number : number + 1] for number in range(12)]
    return (*rows[:7], jnp.concatenate(rows[7:11], 1), rows[11])


def contract_rows(left_mat, right_mat):
    return lax.dot_general(
        left_mat, right_mat, (((0,), (0,)), ((), ())), preferred_element_type=jnp.float32
    )


def contract_cols(left_mat, right_mat):
    return lax.dot_general(
        left_mat, right_mat, (((1,), (1,)), ((), ())), preferred_element_type=jnp.float32
    )


def plain_dot(left_mat, right_mat):
    return jnp.dot(left_mat, right_mat, preferred_element_type=jnp.float32)


def with_other(*values):
    joined = jnp.concatenate(values, 1)
    return jnp.concatenate([joined, swapped(joined, "section")], 0)


def own_half(values):
    half = values.shape[1] // 2
    return lax.dynamic_slice_in_dim(values, lax.axis_index("section") * half, half, 1)


def other_half(values):
    half = values.shape[1] // 2
    return lax.dynamic_slice_in_dim(values, (1 - lax.axis_index("section")) * half, half, 1)


def largest(values):
    return jnp.max(jnp.abs(values)).astype(jnp.float32)


def gelu_tanh(values):
    return jax.nn.gelu(values, approximate=True)


def layer_forward(inputs, weights):
    qkv_t, proj_t, fc_t, down_t, vectors = weights
    g_one, b_one, q_bias, v_bias, p_bias, g_two, b_two, f_bias, d_bias = split_vectors(vectors)
    seq_len, model_width = inputs.shape
    head_count = model_width // HD
    factor = HD ** (-0.5)
    normed_a = layer_norm(inputs, g_one, b_one).astype(jnp.bfloat16)
    bias_qkv = jnp.concatenate([q_bias, jnp.zeros_like(q_bias), v_bias], 1)
    qkv_rows = (contract_cols(normed_a, qkv_t) + bias_qkv).astype(jnp.bfloat16)
    queries = qkv_rows[:, :model_width].reshape(seq_len, head_count, HD)
    keys_all = qkv_rows[:, model_width : 2 * model_width].reshape(seq_len, head_count, HD)
    values_all = qkv_rows[:, 2 * model_width :].reshape(seq_len, head_count, HD)
    scores = (
        jnp.einsum("qhd,khd->hqk", queries, keys_all, preferred_element_type=jnp.float32) * factor
    )
    causal = lax.broadcasted_iota(jnp.int32, (seq_len, seq_len), 0) >= lax.broadcasted_iota(
        jnp.int32, (seq_len, seq_len), 1
    )
    attn_probs = jax.nn.softmax(jnp.where(causal, scores, NEG_FILL), axis=-1)
    probs_low = attn_probs.astype(jnp.bfloat16)
    attended = jnp.einsum("hqk,khd->qhd", probs_low, values_all, preferred_element_type=jnp.float32)
    attended = attended.reshape(seq_len, model_width).astype(jnp.bfloat16)
    after_attn = inputs + contract_cols(attended, proj_t) + p_bias
    normed_b = layer_norm(after_attn, g_two, b_two).astype(jnp.bfloat16)
    hidden_pre = contract_cols(normed_b, fc_t) + f_bias
    hidden_low = gelu_tanh(hidden_pre).astype(jnp.bfloat16)
    outputs = after_attn + plain_dot(hidden_low, down_t) + d_bias
    saved = (
        inputs,
        normed_a,
        queries,
        keys_all,
        values_all,
        attn_probs,
        probs_low,
        attended,
        after_attn,
        normed_b,
        hidden_pre,
        with_other(hidden_low, normed_a, attended, normed_b),
    )
    return (outputs, saved)


def layer_backward(saved, grad_out, weights, nothing):
    qkv_t, proj_t, fc_t, down_t, vectors = weights
    g_one, b_one, q_bias, v_bias, p_bias, g_two, b_two, f_bias, d_bias = split_vectors(vectors)
    (
        inputs,
        normed_a,
        queries,
        keys_all,
        values_all,
        attn_probs,
        probs_low,
        attended,
        after_attn,
        normed_b,
        hidden_pre,
        early,
    ) = saved
    seq_len, model_width = inputs.shape
    factor = HD ** (-0.5)
    grad_mlp = grad_out.astype(jnp.bfloat16)
    d_dbias = jnp.sum(grad_mlp, 0, keepdims=True, dtype=jnp.float32)
    grad_hidden = contract_cols(grad_mlp, down_t)
    grad_pre = jax.vjp(gelu_tanh, hidden_pre)[1](grad_hidden)[0].astype(jnp.bfloat16)
    d_fbias = jnp.sum(grad_pre, 0, keepdims=True, dtype=jnp.float32)
    grad_nb = plain_dot(grad_pre, fc_t)
    ln_two = jax.vjp(layer_norm, after_attn, g_two, b_two)[1](grad_nb)
    grad_mid = grad_out + ln_two[0]
    grad_attn = grad_mid.astype(jnp.bfloat16)
    d_pbias = jnp.sum(grad_attn, 0, keepdims=True, dtype=jnp.float32)
    grad_att = plain_dot(grad_attn, proj_t).reshape(queries.shape).astype(jnp.bfloat16)
    grad_probs = jnp.einsum(
        "qhd,khd->hqk", grad_att, values_all, preferred_element_type=jnp.float32
    )
    grad_vals = jnp.einsum("hqk,qhd->khd", probs_low, grad_att, preferred_element_type=jnp.float32)
    grad_scores = attn_probs * (grad_probs - jnp.sum(grad_probs * attn_probs, -1, keepdims=True))
    grad_scores = grad_scores.astype(jnp.bfloat16)
    grad_q = (
        jnp.einsum("hqk,khd->qhd", grad_scores, keys_all, preferred_element_type=jnp.float32)
        * factor
    )
    grad_k = (
        jnp.einsum("hqk,qhd->khd", grad_scores, queries, preferred_element_type=jnp.float32)
        * factor
    )
    grad_qkv = jnp.concatenate(
        [
            grad_q.reshape(seq_len, model_width),
            grad_k.reshape(seq_len, model_width),
            grad_vals.reshape(seq_len, model_width),
        ],
        -1,
    ).astype(jnp.bfloat16)
    qkv_sums = jnp.sum(grad_qkv, 0, keepdims=True, dtype=jnp.float32)
    late = with_other(grad_qkv + nothing, grad_attn, grad_pre, grad_mlp)
    wide = hidden_pre.shape[1]

    def taken(block, start, width):
        return block[:, start : start + width]

    products = (
        (taken(late, 0, 3 * model_width), taken(early, wide, model_width)),
        (taken(late, 3 * model_width, model_width), taken(early, wide + model_width, model_width)),
        (taken(late, 4 * model_width, wide), taken(early, wide + 2 * model_width, model_width)),
        (taken(early, 0, wide), taken(late, 4 * model_width + wide, model_width)),
    )
    bound = late.shape[0] * largest(early) * largest(late)
    exponent = exponent_for(bound)
    scale = jnp.exp2(exponent)
    d_qkv, d_proj, d_fc, d_down = (
        (contract_rows(left, own_half(right)) * scale).astype(jnp.float16)
        for left, right in products
    )
    grad_na = plain_dot(grad_qkv, qkv_t)
    ln_one = jax.vjp(layer_norm, inputs, g_one, b_one)[1](grad_na)
    grad_in = grad_mid + ln_one[0]
    d_vectors = [
        ln_one[1],
        ln_one[2],
        qkv_sums[:, :model_width],
        qkv_sums[:, 2 * model_width :],
        d_pbias,
        ln_two[1],
        ln_two[2],
        *(d_fbias[:, n * model_width : (n + 1) * model_width] for n in range(4)),
        d_dbias,
    ]
    return (grad_in, (d_qkv, d_proj, d_fc, d_down), d_vectors, exponent)


def adam_step(weights_in, gradient, first_mom, second_mom, step_rate):
    first_new = ADAM_ONE * first_mom + (1.0 - ADAM_ONE) * gradient
    second_new = ADAM_TWO * second_mom + (1.0 - ADAM_TWO) * gradient * gradient
    first_hat = first_new / (1.0 - ADAM_ONE**STEP)
    second_hat = second_new / (1.0 - ADAM_TWO**STEP)
    weights_new = weights_in - step_rate * (
        first_hat / (jnp.sqrt(second_hat) + ADAM_EPS) + ADAM_DECAY * weights_in
    )
    return (weights_new, first_new, second_new)


def halves_of(values):
    high = lax.reduce_precision(values, 8, 7)
    return (high.astype(jnp.bfloat16), (values - high).astype(jnp.bfloat16))


def newton_kernel(gram_ref, out_ref, pair_a, pair_b, gram_now, poly, product):
    tile = gram_ref.shape[1]
    count = 3
    width = count * tile
    a, b, c = NEWTON_COEFS
    rows = lax.broadcasted_iota(jnp.int32, (width, width), 0)
    cols = lax.broadcasted_iota(jnp.int32, (width, width), 1)
    diagonal = rows == cols

    def store_pair(pair, values):
        for part in range(3):
            pair[part] = values.astype(jnp.bfloat16)
            values = values - pair[part].astype(jnp.float32)

    def multiply(left, right, write, terms=2):
        for i in range(count):
            row_at = slice(i * tile, (i + 1) * tile)
            for j in range(i, count):
                col_at = slice(j * tile, (j + 1) * tile)
                block = jnp.zeros((tile, tile), jnp.float32)
                for part in reversed(range(terms)):
                    for other in reversed(range(terms - part)):
                        block += plain_dot(left[part, row_at, :], right[other, :, col_at])
                write(row_at, col_at, block)
                if i != j:
                    write(col_at, row_at, block.T)

    def into(ref):
        def write(row_at, col_at, block):
            ref[row_at, col_at] = block

        return write

    for number, (i, j) in enumerate(UPPER):
        row_at, col_at = slice(i * tile, (i + 1) * tile), slice(j * tile, (j + 1) * tile)
        gram_now[row_at, col_at] = gram_ref[number]
        if i != j:
            gram_now[col_at, row_at] = gram_ref[number].T
    full = gram_now[...]
    trace = jnp.sum(jnp.where(diagonal, full, 0.0))
    inverse = 1.0 / (jnp.sqrt(jnp.full((1, 1), trace, jnp.float32)) + 1e-07)
    gram_now[...] = full * (inverse * inverse)

    def step_poly():
        store_pair(pair_a, gram_now[...])
        multiply(pair_a, pair_a, into(poly))
        poly[...] = jnp.where(diagonal, a, 0.0) + b * gram_now[...] + c * poly[...]
        store_pair(pair_b, poly[...])

    def step_gram(terms):
        multiply(pair_a, pair_b, into(gram_now), terms)
        store_pair(pair_a, gram_now[...])
        multiply(pair_a, pair_b, into(gram_now), terms)

    def step_product():
        store_pair(pair_a, product[...])
        multiply(pair_a, pair_b, into(product))

    step_poly()
    step_gram(3)
    product[...] = poly[...]

    @pl.loop(0, 3)
    def _(iteration):
        step_poly()
        step_gram(2)
        step_product()

    step_poly()
    step_product()
    out_ref[...] = product[...] * inverse


def newton_product(gram_blocks):
    width = 3 * gram_blocks.shape[1]
    square = (width, width)
    return pl.pallas_call(
        newton_kernel,
        out_shape=jax.ShapeDtypeStruct(square, jnp.float32),
        in_specs=[pl.BlockSpec(memory_space=pltpu.VMEM)],
        out_specs=pl.BlockSpec(memory_space=pltpu.VMEM),
        scratch_shapes=[
            pltpu.VMEM((3,) + square, jnp.bfloat16),
            pltpu.VMEM((3,) + square, jnp.bfloat16),
            pltpu.VMEM(square, jnp.float32),
            pltpu.VMEM(square, jnp.float32),
            pltpu.VMEM(square, jnp.float32),
        ],
        compiler_params=pltpu.CompilerParams(vmem_limit_bytes=48 * 1024 * 1024),
        cost_estimate=pl.CostEstimate(
            flops=17 * 4 * width**3, bytes_accessed=8 * width * width, transcendentals=0
        ),
    )(gram_blocks)


def head_forward_kernel(
    shard_rows, spot_ref, one_ref, two_ref, table_ref, target_ref, exp_ref, stat_ref, row_ref
):
    rows = jnp.concatenate([one_ref[0], two_ref[0]], 0)
    row_ref[...] = rows
    logits = contract_cols(rows, table_ref[...])
    cols = lax.broadcasted_iota(jnp.int32, logits.shape, 1)
    logits = jnp.where(cols < shard_rows, logits, NEG_FILL)
    highest = jnp.max(logits, -1, keepdims=True)
    exps = jnp.exp(logits - highest)
    total = jnp.sum(exps, -1, keepdims=True)
    target = jnp.sum(jnp.where(cols == target_ref[...], logits, 0.0), -1, keepdims=True)
    exp_ref[...] = exps.astype(jnp.bfloat16)
    lanes = lax.broadcasted_iota(jnp.int32, stat_ref.shape, 1)
    stat_ref[...] = jnp.where(lanes == 0, highest, jnp.where(lanes == 1, total, target))


def head_forward(blocks, places, table, targets, shard_rows):
    number, tokens, width = blocks.shape
    count = number * tokens
    vocab = table.shape[0]
    step = 2 * tokens
    return pl.pallas_call(
        functools.partial(head_forward_kernel, shard_rows),
        grid_spec=pltpu.PrefetchScalarGridSpec(
            num_scalar_prefetch=1,
            grid=(number // 2,),
            in_specs=[
                pl.BlockSpec((1, tokens, width), lambda i, spot: (spot[2 * i], 0, 0)),
                pl.BlockSpec((1, tokens, width), lambda i, spot: (spot[2 * i + 1], 0, 0)),
                pl.BlockSpec((vocab, width), lambda i, spot: (0, 0)),
                pl.BlockSpec((step, 1), lambda i, spot: (i, 0)),
            ],
            out_specs=[
                pl.BlockSpec((step, vocab), lambda i, spot: (i, 0)),
                pl.BlockSpec((step, 128), lambda i, spot: (i, 0)),
                pl.BlockSpec((step, width), lambda i, spot: (i, 0)),
            ],
        ),
        out_shape=[
            jax.ShapeDtypeStruct((count, vocab), jnp.bfloat16),
            jax.ShapeDtypeStruct((count, 128), jnp.float32),
            jax.ShapeDtypeStruct((count, width), jnp.bfloat16),
        ],
        compiler_params=pltpu.CompilerParams(vmem_limit_bytes=VMEM_BYTES),
        cost_estimate=pl.CostEstimate(
            flops=2 * count * vocab * width,
            bytes_accessed=2 * (vocab * width + count * (width + vocab)),
            transcendentals=count * vocab,
        ),
    )(places, blocks, blocks, table, targets)


def head_pull_kernel(exp_ref, target_ref, table_ref, soft_ref, hard_ref):
    exps = exp_ref[...]
    cols = lax.broadcasted_iota(jnp.int32, exps.shape, 1)
    chosen = jnp.where(cols == target_ref[...], 1.0, 0.0).astype(jnp.bfloat16)
    soft_ref[...] = plain_dot(exps, table_ref[...]).astype(jnp.bfloat16)
    hard_ref[...] = plain_dot(chosen, table_ref[...]).astype(jnp.bfloat16)


def head_pull(exps, targets, table):
    count, vocab = exps.shape
    width = table.shape[1]
    step = min(256, count)
    return pl.pallas_call(
        head_pull_kernel,
        grid=(count // step,),
        out_shape=[
            jax.ShapeDtypeStruct((count, width), jnp.bfloat16),
            jax.ShapeDtypeStruct((count, width), jnp.bfloat16),
        ],
        in_specs=[
            pl.BlockSpec((step, vocab), lambda i: (i, 0)),
            pl.BlockSpec((step, 1), lambda i: (i, 0)),
            pl.BlockSpec((vocab, width), lambda i: (0, 0)),
        ],
        out_specs=[
            pl.BlockSpec((step, width), lambda i: (i, 0)),
            pl.BlockSpec((step, width), lambda i: (i, 0)),
        ],
        compiler_params=pltpu.CompilerParams(vmem_limit_bytes=VMEM_BYTES),
        cost_estimate=pl.CostEstimate(
            flops=4 * count * vocab * width,
            bytes_accessed=2 * (vocab * width + count * (3 * width + vocab)),
            transcendentals=0,
        ),
    )(exps, targets, table)


def head_table_kernel(exp_ref, token_ref, target_ref, row_ref, grad_ref):
    exps = exp_ref[...].astype(jnp.float32)
    cols = lax.broadcasted_iota(jnp.int32, exps.shape, 1)
    at_target = jnp.where(cols == target_ref[...], token_ref[:, 1:2], 0.0)
    grad_logit = (exps * token_ref[:, 0:1] - at_target).astype(jnp.bfloat16)

    @pl.when(pl.program_id(0) == 0)
    def _():
        grad_ref[...] = jnp.zeros_like(grad_ref)

    grad_ref[...] += contract_rows(grad_logit, row_ref[...])


def head_table(exps, token_scales, targets, rows):
    count, vocab = exps.shape
    width = rows.shape[1]
    step = min(256, count)
    return pl.pallas_call(
        head_table_kernel,
        grid=(count // step,),
        out_shape=jax.ShapeDtypeStruct((vocab, width), jnp.float32),
        in_specs=[
            pl.BlockSpec((step, vocab), lambda i: (i, 0)),
            pl.BlockSpec((step, 2), lambda i: (i, 0)),
            pl.BlockSpec((step, 1), lambda i: (i, 0)),
            pl.BlockSpec((step, width), lambda i: (i, 0)),
        ],
        out_specs=pl.BlockSpec((vocab, width), lambda i: (0, 0)),
        compiler_params=pltpu.CompilerParams(vmem_limit_bytes=VMEM_BYTES),
        cost_estimate=pl.CostEstimate(
            flops=2 * count * vocab * width,
            bytes_accessed=2 * (2 * vocab * width + count * (width + vocab)),
            transcendentals=0,
        ),
    )(exps, token_scales, targets, rows)


def row_scatter_kernel(id_ref, part_ref, total_ref, out_ref):
    @pl.when(pl.program_id(0) == 0)
    def _():
        out_ref[...] = total_ref[...]

    spots = lax.broadcasted_iota(jnp.int32, (out_ref.shape[0], id_ref.shape[1]), 0)
    chosen = jnp.where(spots == id_ref[...], 1.0, 0.0).astype(jnp.bfloat16)
    out_ref[...] += plain_dot(chosen, part_ref[...])


def rows_scattered(total, ids, parts):
    vocab, width = total.shape
    count = parts.shape[0]
    step = min(256, count)
    return pl.pallas_call(
        row_scatter_kernel,
        grid=(count // step,),
        out_shape=jax.ShapeDtypeStruct(total.shape, total.dtype),
        input_output_aliases={2: 0},
        in_specs=[
            pl.BlockSpec((1, step), lambda i: (0, i)),
            pl.BlockSpec((step, width), lambda i: (i, 0)),
            pl.BlockSpec((vocab, width), lambda i: (0, 0)),
        ],
        out_specs=pl.BlockSpec((vocab, width), lambda i: (0, 0)),
        compiler_params=pltpu.CompilerParams(vmem_limit_bytes=VMEM_BYTES),
        cost_estimate=pl.CostEstimate(
            flops=2 * count * vocab * width,
            bytes_accessed=8 * vocab * width + 2 * count * width,
            transcendentals=0,
        ),
    )(ids.reshape(1, count), parts, total)


def to_spots(matrices, code):
    widest = max(matrix.shape[0] for matrix in matrices)
    padded = jnp.stack([jnp.pad(m, ((0, widest - m.shape[0]), (0, 0))) for m in matrices])
    padded = padded.reshape(4, 2, widest // 2, -1)
    if code:
        padded = jnp.pad(padded, ((0, 0), (0, 0), (0, NOTE), (0, 0)))
        padded = coded(padded, exponent_for(jnp.max(jnp.abs(padded))))
    sent = lax.all_to_all(padded, "section", 1, 1, tiled=True)
    sent = sent.reshape((-1,) + sent.shape[2:])
    return lax.all_to_all(sent, SPOTS, 0, 0, tiled=True), sent


def at_spots(held, code):
    if code:
        exponents = held[:, -1:, :1].astype(jnp.float32)
        held = held[:, :-NOTE].astype(jnp.float32) * jnp.exp2(-exponents)
    return held.reshape(-1, held.shape[2])


def from_spots(held):
    back = lax.all_to_all(held.reshape(8, -1, held.shape[1]), SPOTS, 0, 0, tiled=True)
    back = back.reshape((4, 2) + back.shape[1:])
    back = lax.all_to_all(back, "section", 1, 1, tiled=True)
    return back.reshape(4, -1, back.shape[3])


def shards(
    token_ids,
    target_ids,
    true_counts,
    embed_table,
    embed_m,
    embed_v,
    pos_table,
    pos_m,
    pos_v,
    w_qkv,
    w_proj,
    w_fc,
    w_down,
    mom_qkv,
    mom_proj,
    mom_fc,
    mom_down,
    layer_vecs,
    vecs_m,
    vecs_v,
    final_norm,
    norm_m,
    norm_v,
):
    section_index = lax.axis_index("section")
    section_count = lax.axis_size("section")
    fsdp_count = lax.axis_size(FSDP)
    shard_rows, model_width = embed_table.shape
    vocab_start = lax.axis_index(FSDP) * shard_rows
    vocab_rows = -(-shard_rows // 128) * 128
    table_rows = jnp.pad(embed_table.astype(jnp.bfloat16), ((0, vocab_rows - shard_rows), (0, 0)))
    masters_t = [w[0].T for w in (w_qkv, w_proj, w_fc, w_down)]
    moments_t = [m[0].T for m in (mom_qkv, mom_proj, mom_fc, mom_down)]
    widths = [w.shape[0] for w in masters_t]
    starts = [sum(widths[:number]) for number in range(5)]
    layer_rows, place_rows = layer_vecs.shape[1], pos_table.shape[0]
    norm_at = section_count * layer_rows
    places_at = norm_at + final_norm.shape[0]
    small_rows = -(-(places_at + place_rows) // 16) * 16

    def padded_rows(parts):
        missing = small_rows - sum(part.shape[0] for part in parts)
        return jnp.concatenate(parts + [jnp.zeros((missing, parts[0].shape[1]), parts[0].dtype)], 0)

    vecs_both = lax.all_gather(layer_vecs[0].astype(jnp.bfloat16), "section", axis=0, tiled=True)
    token_row = jnp.concatenate([token_ids[0], target_ids[0]], 1)
    token_row = jnp.concatenate([token_row // 256, token_row % 256], 1)
    lanes = layer_vecs.shape[2]
    token_rows = -(-token_row.shape[1] // lanes)
    token_row = jnp.pad(token_row, ((0, 0), (0, token_rows * lanes - token_row.shape[1])))
    token_row = token_row.reshape(token_rows, lanes).astype(jnp.bfloat16)
    small = padded_rows([vecs_both, final_norm.astype(jnp.bfloat16), pos_table.astype(jnp.bfloat16)])
    small = spread_small(jnp.concatenate([small, token_row], 0))
    ids_parts = small[:, small_rows:].astype(jnp.int32).reshape(fsdp_count, -1)
    seq_len = token_ids.shape[2]
    ids_targets = 256 * ids_parts[:, : 2 * seq_len] + ids_parts[:, 2 * seq_len : 4 * seq_len]
    ids_all, targets_all = ids_targets[:, :seq_len], ids_targets[:, seq_len:]
    seq_count = ids_all.shape[0]
    small = jnp.moveaxis(small[:, :small_rows], 0, 1).reshape(small_rows, model_width)
    small = small.astype(jnp.float32)
    head_norm = small[norm_at:places_at]
    positions = small[places_at : places_at + place_rows]
    pack = jnp.concatenate(masters_t, 0).astype(jnp.bfloat16)
    local_ids = ids_all - vocab_start
    inside = (local_ids >= 0) & (local_ids < shard_rows)
    safe_ids = jnp.clip(local_ids, 0, shard_rows - 1)
    contrib = jnp.where(
        inside[..., None], jnp.take(table_rows, safe_ids, axis=0), jnp.zeros((), jnp.bfloat16)
    )
    first_side = section_index == 0
    kept_half = own_half(pack)
    came_half = swapped(other_half(pack), "section")
    blocks = [jnp.where(section_index == layer, kept_half, came_half) for layer in range(2)]
    column_early = after(column_near(blocks[0]), small)
    column_late = column_near(after(lax.optimization_barrier(blocks[1]), contrib))
    rows_plane = planes_reduced(planes_cut(contrib), lax.add)
    planes = [planes_near(plane_near(column_early))]
    planes.append(planes_near(plane_near(after(column_late, rows_plane))))
    rows_in = column_sums(plane_reduced(rows_plane, lax.add))
    layer_sets = []
    for layer, own in enumerate(planes):
        other = [swapped(piece, "section") for piece in own]
        layer_sets.append(
            list(assembled(own, other, widths))
            + [small[layer * layer_rows : (layer + 1) * layer_rows]]
        )


    current = rows_in + positions
    kept = []
    for weights in layer_sets:
        current, saved = layer_forward(current, weights)
        kept.append(saved)
    final_rows = current
    normed_low = layer_norm(final_rows, head_norm[0:1], head_norm[1:2]).astype(jnp.bfloat16)
    blocks = jnp.concatenate(gathered_near(normed_low), 0).reshape((fsdp_count,) + normed_low.shape)
    counts_row = jnp.take(true_counts, section_index, axis=0)
    counted = lax.broadcasted_iota(jnp.int32, (seq_count, seq_len), 1) < counts_row[:, None]
    counted = counted.astype(jnp.float32).reshape(-1)
    token_total = jnp.sum(true_counts).astype(jnp.float32)
    local_targets = targets_all.reshape(-1) - vocab_start
    targets_here = (local_targets >= 0) & (local_targets < shard_rows)
    targets_col = jnp.where(targets_here, local_targets, -1)[:, None]
    exps, stats, rows_all = head_forward(
        blocks, places_near(section_index), table_rows, targets_col, shard_rows
    )
    stats = stats[:, :3].T
    block_max, target_logit = stats[0], stats[2]
    stats = spread_small(stats)
    soft_pull, hard_pull = head_pull(exps, targets_col, table_rows)
    moments_sent = [after(moment, blocks) for moment in moments_t]
    held_moments = at_spots(to_spots(moments_sent, True)[0], True)
    highest = jnp.max(stats[:, 0], 0)
    merged_sum = jnp.sum(stats[:, 1] * jnp.exp(stats[:, 0] - highest), 0)
    partition = highest + jnp.log(merged_sum)
    target_all = jnp.sum(stats[:, 2], 0)
    loss_part = jnp.sum(counted * (partition - target_all + Z_WEIGHT * partition * partition))
    token_weight = counted / token_total
    pull = token_weight * (1.0 + 2.0 * Z_WEIGHT * partition) * jnp.exp(block_max - partition)
    token_scales = jnp.stack([pull, token_weight], 1)
    z_pull = token_weight * (1.0 + 2.0 * Z_WEIGHT * partition)
    at_target = z_pull * jnp.exp(target_all - partition) - token_weight
    at_target = lax.reduce_precision(at_target, 8, 7)
    in_soft = jnp.where(targets_here, jnp.exp(target_logit - block_max), 0.0)
    hard_scale = at_target - pull * lax.reduce_precision(in_soft, 8, 7)
    hard_scale = after(hard_scale, held_moments)
    grad_rows = pull[:, None] * soft_pull.astype(jnp.float32) + hard_scale[:, None] * (
        hard_pull.astype(jnp.float32)
    )
    grad_parts = lax.all_to_all(
        grad_rows.astype(jnp.bfloat16).reshape(fsdp_count, -1, model_width), FSDP, 0, 0, tiled=True
    )
    table_grad = head_table(exps, token_scales, targets_col, rows_all)
    grad_parts = after(grad_parts, table_grad)
    grad_normed = jnp.sum(grad_parts, 0, dtype=jnp.float32)
    grad_now, d_fgain, d_fbias = jax.vjp(layer_norm, final_rows, head_norm[0:1], head_norm[1:2])[1](
        grad_normed
    )
    planes_part, vecs_parts = [], []
    nothing = jnp.zeros((), jnp.bfloat16)
    for layer in reversed(range(section_count)):
        grad_now, grads, d_vectors, exponent = layer_backward(
            kept[layer], grad_now, layer_sets[layer], nothing
        )
        parted = parted_weights(grads, exponent)
        planes_part.insert(0, planes_reduced(parted, added))
        if layer:
            grad_now = after(grad_now, parted[-1])
            column_late = plane_reduced(planes_part[0], added)
            parts_late = column_parts(column_late)
            nothing = nothing_of(column_late).astype(jnp.bfloat16)
        vecs_parts = d_vectors + vecs_parts
    emb_all = lax.all_gather(grad_now.astype(jnp.bfloat16), FSDP, axis=0, tiled=True)
    small_grad = lax.optimization_barrier(padded_rows(vecs_parts + [d_fgain, d_fbias, grad_now]))
    small_grad = jnp.moveaxis(small_grad.reshape(small_rows, fsdp_count, -1), 1, 0)
    small_grad = jnp.sum(lax.all_to_all(small_grad, FSDP, 0, 0, tiled=True), 0)
    column_early = plane_reduced(planes_part[0], added)
    parts_early = column_parts(column_early)
    late_ids = local_ids.reshape(-1) + nothing_of(column_early, small_grad, *parts_late).astype(
        jnp.int32
    )
    table_grad = rows_scattered(table_grad, late_ids, emb_all)
    table_grad = (table_grad + swapped(table_grad, "section"))[:shard_rows]
    own_rows = shard_rows // section_count
    table_part = lax.dynamic_slice_in_dim(table_grad, section_index * own_rows, own_rows, 0)
    table_squares = jnp.sum(table_part * table_part)
    flushed = summed_weights(parts_early, parts_late, table_squares)
    loss_row = jnp.broadcast_to(loss_part, (1, small_grad.shape[1]))
    small_grad = jnp.concatenate([small_grad, loss_row], 0)
    small_grad = small_grad + swapped(small_grad, "section")
    loss_sum = small_grad[-1, 0]
    vecs_grad = lax.dynamic_slice_in_dim(small_grad, section_index * layer_rows, layer_rows, 0)
    norm_grad = small_grad[norm_at:places_at]
    pos_grad = small_grad[places_at : places_at + place_rows]
    weight_grad = flushed
    held_grads, set_out = to_spots([weight_grad[starts[n] : starts[n + 1]] for n in range(4)], True)
    held_grads = at_spots(held_grads, True)
    own_squares = jnp.sum(weight_grad * weight_grad) + jnp.sum(vecs_grad * vecs_grad)
    shared_squares = jnp.sum(pos_grad * pos_grad) + jnp.sum(norm_grad * norm_grad)
    device_squares = (
        own_squares + table_squares + jnp.where(section_index == 0, shared_squares, 0.0)
    )
    square_sum = lax.psum(
        jnp.sum(spread_small(jnp.full((8, 128), device_squares)), 0)[0, 0], "section"
    )
    clip_norm = jnp.sqrt(square_sum)
    factor = jnp.minimum(1.0, CLIP_NORM / (clip_norm + 1e-06))

    new_moms = [
        MOMENTUM * moments_t[n] + factor * weight_grad[starts[n] : starts[n + 1]] for n in range(4)
    ]
    held = MOMENTUM * held_moments + factor * held_grads
    high, lower = halves_of(held)
    gram = contract_rows(
        jnp.concatenate([lower, lower, high, high]), jnp.concatenate([lower, high, lower, high])
    )
    product = newton_product(gram_summed(gram))
    turned = jnp.matmul(held, product, precision=lax.Precision.HIGH).astype(jnp.float16)
    back = from_spots(turned)
    back = back.astype(jnp.float32)

    embed_new, embed_m_new, embed_v_new = adam_step(
        embed_table, factor * table_grad, embed_m, embed_v, RATE_EMBED
    )
    pos_new, pos_m_new, pos_v_new = adam_step(pos_table, factor * pos_grad, pos_m, pos_v, RATE_POS)
    norm_new, norm_m_new, norm_v_new = adam_step(
        final_norm, factor * norm_grad, norm_m, norm_v, RATE_VEC
    )
    vecs_new, vecs_m_new, vecs_v_new = adam_step(
        layer_vecs, factor * vecs_grad[None], vecs_m, vecs_v, RATE_VEC
    )
    results = []
    for number in range(4):
        column_factor = math.sqrt(widths[number] * fsdp_count / model_width)
        new_master = masters_t[number] - MUON_RATE * (
            column_factor * back[number, : widths[number]] + MUON_DECAY * masters_t[number]
        )
        new_master = new_master.T[None]
        results.append((new_master, new_master.astype(jnp.bfloat16), new_moms[number].T[None]))
    return (
        loss_sum,
        clip_norm,
        embed_new,
        embed_new.astype(jnp.bfloat16),
        embed_m_new,
        embed_v_new,
        pos_new,
        pos_m_new,
        pos_v_new,
        *results[0],
        *results[1],
        *results[2],
        *results[3],
        vecs_new,
        vecs_m_new,
        vecs_v_new,
        norm_new,
        norm_m_new,
        norm_v_new,
    )


def inner_mesh(mesh):
    section_count, fsdp_count = mesh.devices.shape
    parts = {16: (4, 2, 1, 2), 64: (4, 2, 2, 4)}.get(fsdp_count, (4, 2, fsdp_count // 8, 1))
    return Mesh(mesh.devices.reshape((section_count,) + parts), ("section",) + FSDP)


def solution(mesh):
    ids = P("section", FSDP, None)
    rows = P(FSDP, None)
    cols = P(None, FSDP)
    layer = P("section", None, FSDP)
    in_specs = (ids, ids, P()) + (rows,) * 3 + (cols,) * 3 + (layer,) * 11 + (cols,) * 3
    out_specs = (P(), P()) + (rows,) * 4 + (cols,) * 3 + (layer,) * 15 + (cols,) * 3
    return jax.shard_map(
        shards, mesh=inner_mesh(mesh), in_specs=in_specs, out_specs=out_specs, check_vma=False
    )
```
